512 devices in a mesh: seq: 16 (over x, y_lo, core), fsdp: 16 (over z), batch: 2 (over y_hi).
Axes of the slice: x: 4, y: 4 (y_hi: 2, y_lo: 2; y = y_hi * 2 + y_lo), z: 16, core: 2. Of those that a mesh axis runs over, the one named last changes fastest.
Arguments:
- ssm_input: bfloat16 [49152, 8192], P(('batch', 'seq', 'fsdp')), parts along dimension 0, may hold values from -6 to 6
- gate_input: bfloat16 [49152, 8192], P(('batch', 'seq', 'fsdp')), parts along dimension 0, may hold values from -6 to 6
- coupling: bfloat16 [49152, 2048], P(('batch', 'seq', 'fsdp')), parts along dimension 0, may hold values from -6 to 6
- step_input: bfloat16 [49152, 128], P(('batch', 'seq', 'fsdp')), parts along dimension 0, may hold values from -4 to 4
- conv_input: bfloat16 [4, 8192], P(None, 'fsdp'), may hold values from -3 to 3
- conv_coupling: bfloat16 [4, 2048], P(None, 'fsdp'), may hold values from -3 to 3
- step_bias: float32 [128], P('fsdp'), may hold values from -8 to 1.1
- log_rate: float32 [128], P('fsdp'), may hold values from -6 to -3.2
- skip_gain: float32 [128], P('fsdp'), may hold values from 0.5 to 1.5
- norm_gain: bfloat16 [8192], replicated, may hold values from 0.5 to 1.5
Outputs:
- layer_out: bfloat16 [49152, 8192], P(('batch', 'seq', 'fsdp')), parts along dimension 0
The draws below stay inside these ranges and needn't reach their ends.
There are 2 independent parts, one for each index of `batch`. The reference program is written for one: setup_inputs(seed, part) draws one part's arguments, and reference() takes and returns one part's arrays. A program takes and returns all parts, laid end to end along the dimension named above; an argument that names none is the same for every part. Nothing has to cross between parts.
All inputs are finite; a program needn't handle non-finite values.
Results may differ from the reference program's by a relative error of at most 0.0051.
Values may be sent and summed in bfloat16 or wider, within the bound.
No kernel may reach another device: no remote copies, remote signals or barrier semaphores. Data moves between devices by JAX's collectives and lax.ppermute only.
A program may use at most 64 MiB of HBM per device.

```python
import jax
import jax.numpy as jnp
from jax import lax

HEADS = 128
HEAD_DIM = 64
STATE = 256
GROUP_HEADS = 32
KERNEL = 4
GROUPS = 4
SEQ_TOKENS = 24576


def head_law(key):
    key_fast, key_short, key_long = jax.random.split(jax.random.fold_in(key, 11), 3)
    fast_share = 0.5
    is_fast = jax.random.uniform(key_fast, (HEADS,), jnp.float32) < fast_share
    short_window = jnp.exp(jax.random.uniform(key_short, (HEADS,), jnp.float32, jnp.log(20.0), jnp.log(40.0)))
    long_window = SEQ_TOKENS * jnp.exp(jax.random.uniform(key_long, (HEADS,), jnp.float32, jnp.log(2.0), jnp.log(8.0)))
    window = jnp.where(is_fast, short_window, long_window)
    step_level = (30.0 / window) ** 0.75
    step_offset = jnp.log(jnp.expm1(step_level))
    log_rate = -jnp.log(window * step_level)
    return (step_offset, log_rate)


def draw_step_bias(key, part):
    return head_law(key)[0].astype(jnp.float32)


def draw_log_rate(key, part):
    return head_law(key)[1].astype(jnp.float32)


def levels(own_key, dims, pieces, least, high):
    level = 1.0
    for dim, shards_of in pieces:
        draws = jax.random.uniform(jax.random.fold_in(jax.random.fold_in(own_key, 6), dim), (shards_of,), jnp.float32, least / len(pieces), high / len(pieces))
        level = level * jnp.repeat(jnp.exp(draws), dims[dim] // shards_of).reshape((-1,) + (1,) * (len(dims) - 1 - dim))
    return level


def bell_draw(own_key, dims, deviation, bound, shards=(), kind=jnp.bfloat16):
    gain = levels(own_key, dims, shards, -0.22, 0.18) if shards else 1.0
    result = jax.random.normal(own_key, dims, jnp.float32) * deviation * gain
    return jnp.minimum(jnp.maximum(result, -bound), bound).astype(kind)


def setup_inputs(seed: int = 0, part: int = 0) -> dict:
    keys = jax.random.split(jax.random.key(seed), 11)
    own_keys = jax.random.split(jax.random.fold_in(keys[10], part), 11)
    ssm_input = bell_draw(own_keys[0], (SEQ_TOKENS, HEADS * HEAD_DIM), 1.0, 6.0, ((0, 256),))
    gate_input = bell_draw(own_keys[1], (SEQ_TOKENS, HEADS * HEAD_DIM), 1.0, 6.0, ((0, 256),))
    coupling = bell_draw(own_keys[2], (SEQ_TOKENS, 2 * GROUPS * STATE), 1.0, 6.0, ((0, 256),))
    step_input = bell_draw(own_keys[3], (SEQ_TOKENS, HEADS), 0.8, 4.0, ((0, 256),))
    conv_input = bell_draw(keys[4], (KERNEL, HEADS * HEAD_DIM), KERNEL ** -0.5, 3.0, ((1, 16),))
    conv_coupling = bell_draw(keys[5], (KERNEL, 2 * GROUPS * STATE), KERNEL ** -0.5, 3.0, ((1, 16),))
    step_bias = draw_step_bias(jax.random.fold_in(keys[10], 71), part)
    log_rate = draw_log_rate(jax.random.fold_in(keys[10], 71), part)
    skip_gain = jnp.clip(0.5 + 1.0 * jax.random.uniform(keys[8], (HEADS,), jnp.float32) ** levels(keys[8], (HEADS,), ((0, 16),), -0.2, 0.2), 0.5, 1.5)
    norm_gain = jnp.clip(1.0 + 0.1 * jax.random.normal(keys[9], (HEADS * HEAD_DIM,), jnp.float32), 0.5, 1.5).astype(jnp.bfloat16)
    return dict(ssm_input=ssm_input, gate_input=gate_input, coupling=coupling, step_input=step_input, conv_input=conv_input, conv_coupling=conv_coupling, step_bias=step_bias, log_rate=log_rate, skip_gain=skip_gain, norm_gain=norm_gain)


precise = lax.Precision.HIGHEST

def conv_block(raw_rows, tail_rows, weights):
    extended = jnp.concatenate([tail_rows, raw_rows], axis=0).astype(jnp.float32)
    weights_wide = weights.astype(jnp.float32)
    kernel_len = weights.shape[0]
    row_count = raw_rows.shape[0]
    summed = extended[0:row_count] * weights_wide[0][None, :]
    for offset in range(1, kernel_len):
        summed = summed + extended[offset:offset + row_count] * weights_wide[offset][None, :]
    return jax.nn.silu(summed).astype(jnp.bfloat16)

def scan_block(carried, inputs, read_in, read_out, step_sizes, decay_rate, skip_gain, group_span):
    log_decay = -decay_rate[None, :] * step_sizes
    cumulated = jnp.cumsum(log_decay, axis=0)
    intersection = jnp.einsum('ign,jgn->gij', read_out, read_in, precision=precise)
    intersection = jnp.repeat(intersection, group_span, axis=0)
    gap_log = cumulated.T[:, :, None] - cumulated.T[:, None, :]
    length = inputs.shape[0]
    lower_mask = (jnp.arange(length)[:, None] >= jnp.arange(length)[None, :])[None]
    decay_mat = jnp.where(lower_mask, jnp.exp(jnp.where(lower_mask, gap_log, 0.0)), 0.0)
    mixing = intersection * decay_mat * step_sizes.T[:, None, :]
    intra_out = jnp.einsum('hij,jhp->ihp', mixing, inputs, precision=precise)
    heads_out = jnp.repeat(read_out, group_span, axis=1)
    carry_out = jnp.exp(cumulated)[:, :, None] * jnp.einsum('ihn,hpn->ihp', heads_out, carried, precision=precise)
    heads_in = jnp.repeat(read_in, group_span, axis=1)
    weight_end = jnp.exp(cumulated[-1][None, :] - cumulated) * step_sizes
    updated = jnp.exp(cumulated[-1])[:, None, None] * carried + jnp.einsum('jhp,jhn->hpn', inputs * weight_end[:, :, None], heads_in, precision=precise)
    return (updated, intra_out + carry_out + skip_gain[None, :, None] * inputs, cumulated)

def finish_norm(mixed_rows, gate_rows, gain_row):
    gated = mixed_rows.astype(jnp.float32) * jax.nn.silu(gate_rows.astype(jnp.float32))
    row_count = gated.shape[0]
    grouped = gated.reshape(row_count, GROUPS, -1)
    inv_scale = lax.rsqrt(lax.optimization_barrier(jnp.mean(grouped * grouped, axis=-1, keepdims=True)) + 1e-05)
    normed = (grouped * inv_scale).reshape(row_count, -1)
    return (normed * gain_row.astype(jnp.float32)[None, :]).astype(jnp.bfloat16)

def reference(ssm_input, gate_input, coupling, step_input, conv_input, conv_coupling, step_bias, log_rate, skip_gain, norm_gain):
    block_len = min(512, SEQ_TOKENS)
    block_count = SEQ_TOKENS // block_len
    inner_width = HEADS * HEAD_DIM
    pair_width = GROUPS * STATE
    decay_rate = jnp.exp(log_rate)

    def advance(loop_carry, block_index):
        carried, tail_inputs, tail_coupling = loop_carry
        row_start = block_index * block_len
        raw_inputs = lax.dynamic_slice_in_dim(ssm_input, row_start, block_len, 0)
        raw_coupling = lax.dynamic_slice_in_dim(coupling, row_start, block_len, 0)
        raw_steps = lax.dynamic_slice_in_dim(step_input, row_start, block_len, 0)
        raw_gate = lax.dynamic_slice_in_dim(gate_input, row_start, block_len, 0)
        conv_inputs = conv_block(raw_inputs, tail_inputs, conv_input)
        conv_rows = conv_block(raw_coupling, tail_coupling, conv_coupling)
        inputs = conv_inputs.astype(jnp.float32).reshape(block_len, HEADS, HEAD_DIM)
        read_in = conv_rows[:, :pair_width].astype(jnp.float32).reshape(block_len, GROUPS, STATE)
        read_out = conv_rows[:, pair_width:].astype(jnp.float32).reshape(block_len, GROUPS, STATE)
        step_sizes = jax.nn.softplus(raw_steps.astype(jnp.float32) + step_bias[None, :])
        updated, mixed_out, _ = scan_block(carried, inputs, read_in, read_out, step_sizes, decay_rate, skip_gain, GROUP_HEADS)
        mixed_rows = mixed_out.reshape(block_len, inner_width).astype(jnp.bfloat16)
        finished = finish_norm(mixed_rows, raw_gate, norm_gain)
        next_carry = (updated, raw_inputs[block_len - (KERNEL - 1):], raw_coupling[block_len - (KERNEL - 1):])
        return (next_carry, finished)
    start_carry = (jnp.zeros((HEADS, HEAD_DIM, STATE), jnp.float32), jnp.zeros((KERNEL - 1, inner_width), jnp.bfloat16), jnp.zeros((KERNEL - 1, 2 * pair_width), jnp.bfloat16))
    _, blocks_out = lax.scan(advance, start_carry, jnp.arange(block_count, dtype=jnp.int32))
    return blocks_out.reshape(SEQ_TOKENS, inner_width)
```

```python
import functools

import jax
import jax.numpy as jnp
from jax import lax
from jax.experimental import pallas as pl
from jax.experimental.pallas import tpu as pltpu
from jax.sharding import PartitionSpec as P

HEAD_DIM = 64
STATE = 256
GROUPS = 4
LANES = 128
PARTS = 1
LOG2E = 1.4426950408889634

F32 = jnp.float32
BF16 = jnp.bfloat16
exact = lax.Precision.HIGHEST
params = pltpu.CompilerParams(vmem_limit_bytes=48 * 2**20)


def iota(shape, dim):
    return lax.broadcasted_iota(jnp.int32, shape, dim)


def filtered(scratch, tail, block, taps):
    rows = block.shape[0]
    scratch[0:8] = tail
    scratch[8 : 8 + rows] = block
    total = scratch[5 : 5 + rows] * taps[0:1]
    total = total + scratch[6 : 6 + rows] * taps[1:2]
    total = total + scratch[7 : 7 + rows] * taps[2:3]
    total = total + block * taps[3:4]
    return jax.nn.silu(total).astype(BF16)


def coupling_kernel(raw_ref, tail_ref, taps_ref, out_ref, scratch):
    count, rows, _ = raw_ref.shape
    taps = taps_ref[...].astype(F32)
    scratch[rows : rows + 8] = tail_ref[...]

    def body(c, _):
        out_ref[c] = filtered(scratch, scratch[rows : rows + 8], raw_ref[c].astype(F32), taps)
        return 0

    lax.fori_loop(0, count, body, 0)


def decay_tables(steps_ref, bias_ref, log_rate_ref, rows):
    count, heads, lanes = steps_ref.shape
    dt = jax.nn.softplus(steps_ref[...] + bias_ref[...][None])
    log_decay = -jnp.exp(log_rate_ref[...])[None] * dt
    size = (lanes, lanes)
    upper = jnp.where(iota(size, 0) <= iota(size, 1), 1.0, 0.0).astype(F32)
    flat = log_decay.reshape(count * heads, lanes)
    cum = jnp.dot(flat, upper, precision=exact, preferred_element_type=F32)
    return dt.reshape(count * heads, lanes), cum, cum[:, rows - 1 : rows]


def high_low(table):
    high = table.astype(BF16).astype(F32)
    return high, table - high


def spread_matrix(heads, width, first, copies):
    shape = (copies * heads, width)
    return jnp.where(iota(shape, 0) % heads == first + iota(shape, 1) // HEAD_DIM, 1.0, 0.0).astype(BF16)


def pick(sel_ref, pieces, read_in, read_out):
    half = LANES

    @pl.when(sel_ref[0] == 0)
    def _():
        for k in range(2):
            if read_in is not None:
                read_in[:, :, k * half : (k + 1) * half] = pieces[k][...]
            if read_out is not None:
                read_out[:, :, k * half : (k + 1) * half] = pieces[2 + k][...]

    @pl.when(sel_ref[0] != 0)
    def _():
        for k in range(2):
            if read_in is not None:
                read_in[:, :, k * half : (k + 1) * half] = pieces[2 + k][...]
            if read_out is not None:
                read_out[:, :, k * half : (k + 1) * half] = pieces[k][...]


def state_kernel(first, sel_ref, x_ref, tail_ref, taps_ref, p0, p1, p2, p3, steps_ref, bias_ref, log_rate_ref,
                 xf_ref, state_ref, total_ref, scratch, weighted, read_in, table):
    count, rows, width = x_ref.shape
    heads = steps_ref.shape[1]
    dt, cum, tot = decay_tables(steps_ref, bias_ref, log_rate_ref, rows)
    size = (count * heads, count * heads)
    later_mat = jnp.where(
        (iota(size, 0) % heads == iota(size, 1) % heads) & (iota(size, 1) // heads > iota(size, 0) // heads), 1.0, 0.0
    ).astype(F32)
    later = jnp.dot(later_mat, jnp.broadcast_to(tot, cum.shape), precision=exact, preferred_element_type=F32)
    weight = jnp.exp(later + (tot - cum)) * dt
    high, low = high_low(weight)
    table[:, 0:heads] = high.reshape(count, heads, -1)
    table[:, heads : 2 * heads] = low.reshape(count, heads, -1)
    own = iota((heads, width), 0) == first + iota((heads, width), 1) // HEAD_DIM
    section = tot[0:heads] + later[0:heads, 0:1]
    logs = jnp.sum(jnp.where(own, jnp.broadcast_to(section, own.shape), 0.0), axis=0, keepdims=True)
    high, low = high_low(jnp.broadcast_to(logs, total_ref.shape))
    total_ref[...] = jnp.where(iota(total_ref.shape, 0) == 0, high, low).astype(BF16)
    pick(sel_ref, (p0, p1, p2, p3), read_in, None)
    taps = taps_ref[...].astype(F32)
    spread = spread_matrix(heads, width, first, 2)
    scratch[rows : rows + 8] = tail_ref[...]

    def body(c, _):
        xf = filtered(scratch, scratch[rows : rows + 8], x_ref[c].astype(F32), taps)
        xf_ref[c] = xf
        columns = jnp.transpose(table[c])[:rows].astype(BF16)
        scale = jnp.dot(columns, spread, preferred_element_type=F32)
        weighted[c] = (xf.astype(F32) * scale).astype(BF16)
        return 0

    lax.fori_loop(0, count, body, 0)
    state = lax.dot_general(
        read_in[...].reshape(count * rows, STATE),
        weighted[...].reshape(count * rows, width),
        (((0,), (0,)), ((), ())),
        preferred_element_type=F32,
    )
    state_ref[...] = state.reshape(state_ref.shape).astype(BF16)


def relay_kernel(state_ref, log_ref, out_ref):
    sections = state_ref.shape[0]
    carried = jnp.zeros(state_ref.shape[1:], F32)
    for s in range(sections):
        out_ref[s] = carried.astype(BF16)
        carried = jnp.exp(log_ref[s : s + 1]) * carried + state_ref[s].astype(F32)


def output_kernel(first, sel_ref, xf_ref, p0, p1, p2, p3, steps_ref, bias_ref, log_rate_ref, skip_ref, in_ref,
                  y_ref, state, read_in, read_out, table, column_logs, row_logs):
    count, rows, width = xf_ref.shape
    heads = steps_ref.shape[1]
    dt, cum, tot = decay_tables(steps_ref, bias_ref, log_rate_ref, rows)
    blocked = (count, heads, dt.shape[1])
    w_high, w_low = high_low(jnp.exp(tot - cum) * dt)
    e_high, e_low = high_low(jnp.exp(cum))
    for k, part in enumerate((w_high, w_low, e_high, e_low)):
        table[:, k * heads : (k + 1) * heads] = part.reshape(blocked)
    column_logs[...] = (cum * LOG2E).reshape(blocked)
    row_logs[...] = ((jnp.log(dt) - cum) * LOG2E).reshape(blocked)
    pick(sel_ref, (p0, p1, p2, p3), read_in, read_out)
    spread = spread_matrix(heads, width, first, 2)
    skip = skip_ref[...]
    state[...] = in_ref[...].astype(F32)
    causal = iota((rows, rows), 0) >= iota((rows, rows), 1)
    left = iota((rows, LANES), 1) < HEAD_DIM

    def body(c, _):
        b, q, x = read_in[c], read_out[c], xf_ref[c]
        meet = lax.dot_general(q, b, (((1,), (1,)), ((), ())), preferred_element_type=F32)
        meet = jnp.where(causal, meet, 0.0)
        columns = jnp.transpose(table[c])[:rows].astype(BF16)
        scale_in = jnp.dot(columns[:, : 2 * heads], spread, preferred_element_type=F32)
        scale_out = jnp.dot(columns[:, 2 * heads :], spread, preferred_element_type=F32)
        logs = jnp.transpose(column_logs[c])[:rows]
        rows_c = row_logs[c]
        carried = jnp.dot(q, state[...].astype(BF16), preferred_element_type=F32) * scale_out
        x32 = x.astype(F32)
        for pair in range(width // LANES):
            lanes = slice(pair * LANES, (pair + 1) * LANES)
            both = []
            for k in range(2):
                h = first + 2 * pair + k
                mix = jnp.exp2(logs[:, h : h + 1] + rows_c[h : h + 1, :rows]) * meet
                both.append(jnp.dot(mix.astype(BF16), x[:, lanes], preferred_element_type=F32))
            mixed = jnp.where(left, both[0], both[1])
            y_ref[c, :, lanes] = (mixed + carried[:, lanes] + skip[:, lanes] * x32[:, lanes]).astype(BF16)
        state[...] = state[...] * scale_out[rows - 1 : rows] + lax.dot_general(
            b, (x32 * scale_in).astype(BF16), (((0,), (0,)), ((), ())), preferred_element_type=F32
        )
        return 0

    lax.fori_loop(0, count, body, 0)


def finish_kernel(*refs):
    parts, (gate_ref, gain_ref, out_ref, gated_ref) = refs[:-4], refs[-4:]
    blocks, rows, width = parts[0].shape
    total = jnp.zeros((rows, 1), F32)
    pieces = [(z, p) for z in range(blocks) for p in range(len(parts))]
    for i, (z, p) in enumerate(pieces):
        lanes = slice(i * width, (i + 1) * width)
        gated = parts[p][z].astype(F32) * jax.nn.silu(gate_ref[:, lanes].astype(F32))
        gated_ref[:, lanes] = gated
        total = total + jnp.sum(gated * gated, axis=1, keepdims=True)
    scale = lax.rsqrt(total / (len(pieces) * width) + 1e-05)
    for i in range(len(pieces)):
        lanes = slice(i * width, (i + 1) * width)
        out_ref[:, lanes] = (gated_ref[:, lanes] * scale * gain_ref[:, lanes].astype(F32)).astype(BF16)


def call(kernel, outs, scratch, args, cost=(0, 0), smem_first=False):
    specs = [pl.BlockSpec(memory_space=pltpu.VMEM)] * len(args)
    if smem_first:
        specs[0] = pl.BlockSpec(memory_space=pltpu.SMEM)
    return pl.pallas_call(
        kernel,
        out_shape=outs,
        in_specs=specs,
        out_specs=jax.tree.map(lambda _: pl.BlockSpec(memory_space=pltpu.VMEM), outs),
        scratch_shapes=scratch,
        compiler_params=params,
        cost_estimate=pl.CostEstimate(flops=cost[0], bytes_accessed=cost[1], transcendentals=0),
    )(*args)


def local(
    ssm_input,
    gate_input,
    coupling,
    step_input,
    conv_input,
    conv_coupling,
    step_bias,
    log_rate,
    skip_gain,
    norm_gain,
):
    rows = ssm_input.shape[0]
    ring = lax.axis_size("fsdp")
    heads = step_bias.shape[0]
    width = conv_input.shape[1]
    part_width = width // PARTS
    part_heads = heads // PARTS
    struct = jax.ShapeDtypeStruct

    seq, whole = lax.axis_size("seq"), lax.axis_size("seq") * ring
    last_rows = jnp.concatenate([ssm_input[rows - 3 :], coupling[rows - 3 :]], axis=1)
    tails = lax.ppermute(last_rows, ("seq", "fsdp"), [(i, i + 1) for i in range(whole - 1)])
    taps_route = [(8 * r + 2 * g + k, 4 * g + 2 * r + k) for g in range(GROUPS) for r in range(2) for k in range(2)]
    taps_coupling = lax.ppermute(conv_coupling, "fsdp", taps_route)

    def by_owner(block):
        count = block.shape[0]
        split = block.reshape(count, 2, GROUPS, 2, LANES)
        return split.transpose(2, 1, 3, 0, 4).reshape(ring, count, LANES)

    steps_t = jnp.pad(step_input.T.reshape(ring, heads, rows), ((0, 0), (0, 0), (0, LANES - rows)))
    x_tails = tails[:, : ssm_input.shape[1]].reshape(3, ring, width // LANES, LANES).transpose(1, 2, 0, 3)
    x_tail_rows = 3 * width // LANES
    small = jnp.concatenate(
        [
            by_owner(coupling),
            steps_t,
            x_tails.reshape(ring, x_tail_rows, LANES),
            by_owner(tails[:, ssm_input.shape[1] :]),
            jnp.zeros((ring, 1, LANES), BF16),
        ],
        axis=1,
    )
    small = lax.all_to_all(small, "fsdp", 0, 0)
    x_blocks = ssm_input.reshape(rows, ring, PARTS, part_width)
    x_parts = [lax.all_to_all(x_blocks[:, :, p].transpose(1, 0, 2), "fsdp", 0, 0) for p in range(PARTS)]

    at = rows
    steps = small[:, at : at + heads].astype(F32)
    at += heads
    x_tail = small[0, at : at + x_tail_rows].reshape(width // LANES, 3, LANES).transpose(1, 0, 2).reshape(3, width)
    x_tail = jnp.pad(x_tail.astype(F32), ((5, 0), (0, 0)))
    at += x_tail_rows
    c_tail = jnp.pad(small[0, at : at + 3].astype(F32), ((5, 0), (0, 0)))

    own = call(
        coupling_kernel,
        struct((ring, rows, LANES), BF16),
        [pltpu.VMEM((rows + 8, LANES), F32)],
        (small[:, :rows], c_tail, taps_coupling),
        (4000000, 800000),
    )
    pieces = [own]
    for d in range(1, 4):
        pieces.append(lax.ppermute(own, "fsdp", [(i, i ^ d) for i in range(ring)]))
    select = (lax.axis_index("fsdp") // 2 % 2).astype(jnp.int32).reshape(1)
    bias, rate = step_bias.reshape(heads, 1), log_rate.reshape(heads, 1)
    skip = jnp.repeat(skip_gain, HEAD_DIM).reshape(1, width)

    outs = []
    for p in range(PARTS):
        first = p * part_heads
        lanes = slice(p * part_width, (p + 1) * part_width)
        share = STATE // seq
        xf, state, total = call(
            functools.partial(state_kernel, first),
            (
                struct((ring, rows, part_width), BF16),
                struct((seq, share, part_width), BF16),
                struct((16, part_width), BF16),
            ),
            [
                pltpu.VMEM((rows + 8, part_width), F32),
                pltpu.VMEM((ring, rows, part_width), BF16),
                pltpu.VMEM((ring, rows, STATE), BF16),
                pltpu.VMEM((ring, 2 * heads, LANES), F32),
            ],
            (select, x_parts[p], x_tail[:, lanes], conv_input[:, lanes], *pieces, steps, bias, rate),
            (400000000, 5000000),
            True,
        )
        message = jnp.concatenate([state, jnp.broadcast_to(total[:8], (seq, 8, part_width))], axis=1)
        message = lax.all_to_all(message, "seq", 0, 0)
        section_logs = message[:, share].astype(F32) + message[:, share + 1].astype(F32)
        incoming = call(
            relay_kernel,
            struct((seq, share, part_width), BF16),
            [],
            (message[:, :share], section_logs),
            (1000000, 600000),
        )
        incoming = lax.all_to_all(incoming, "seq", 0, 0).reshape(STATE, part_width)
        y = call(
            functools.partial(output_kernel, first),
            struct((ring, rows, part_width), BF16),
            [
                pltpu.VMEM((STATE, part_width), F32),
                pltpu.VMEM((ring, rows, STATE), BF16),
                pltpu.VMEM((ring, rows, STATE), BF16),
                pltpu.VMEM((ring, 4 * heads, LANES), F32),
                pltpu.VMEM((ring, heads, LANES), F32),
                pltpu.VMEM((ring, heads, LANES), F32),
            ],
            (select, xf, *pieces, steps, bias, rate, skip[:, lanes], incoming),
            (1600000000, 5000000),
            True,
        )
        outs.append(lax.all_to_all(y, "fsdp", 0, 0))

    group_width = ssm_input.shape[1] // GROUPS
    blocks = ring // GROUPS
    return pl.pallas_call(
        finish_kernel,
        grid=(GROUPS,),
        out_shape=struct(ssm_input.shape, BF16),
        in_specs=[pl.BlockSpec((blocks, rows, part_width), lambda g: (g, 0, 0))] * PARTS
        + [
            pl.BlockSpec((rows, group_width), lambda g: (0, g)),
            pl.BlockSpec((1, group_width), lambda g: (0, g)),
        ],
        out_specs=pl.BlockSpec((rows, group_width), lambda g: (0, g)),
        scratch_shapes=[pltpu.VMEM((rows, group_width), F32)],
        compiler_params=params,
    )(*outs, gate_input, norm_gain.reshape(1, -1))


def solution(mesh):
    return jax.shard_map(
        local,
        mesh=mesh,
        in_specs=(
            P(("batch", "seq", "fsdp"), None),
            P(("batch", "seq", "fsdp"), None),
            P(("batch", "seq", "fsdp"), None),
            P(("batch", "seq", "fsdp"), None),
            P(None, "fsdp"),
            P(None, "fsdp"),
            P("fsdp"),
            P("fsdp"),
            P("fsdp"),
            P(),
        ),
        out_specs=P(("batch", "seq", "fsdp"), None),
        check_vma=False,
    )
```

```python
import jax
import jax.numpy as jnp
from jax import lax
from jax.experimental import pallas as pl
from jax.experimental.pallas import tpu as pltpu
from jax.sharding import PartitionSpec as P

HEAD_DIM = 64
STATE = 256
GROUPS = 4
LANES = 128
HALO = 8
LOG2E = 1.4426950408889634

F32 = jnp.float32
BF16 = jnp.bfloat16
exact = lax.Precision.HIGHEST
params = pltpu.CompilerParams(vmem_limit_bytes=48 * 2**20)


def iota(shape, dim):
    return lax.broadcasted_iota(jnp.int32, shape, dim)


def decay_tables(steps_ref, bias_ref, log_rate_ref, rows):
    count, heads, lanes = steps_ref.shape
    dt = jax.nn.softplus(steps_ref[...] + bias_ref[...][None])
    log_decay = -jnp.exp(log_rate_ref[...])[None] * dt
    size = (lanes, lanes)
    upper = jnp.where(iota(size, 0) <= iota(size, 1), 1.0, 0.0).astype(F32)
    flat = log_decay.reshape(count * heads, lanes)
    cum = jnp.dot(flat, upper, precision=exact, preferred_element_type=F32)
    return dt.reshape(count * heads, lanes), cum, cum[:, rows - 1 : rows]


def high_low(table):
    high = table.astype(BF16).astype(F32)
    return high, table - high


def spread_matrix(heads, width, copy):
    shape = (LANES, width)
    row, lane = iota(shape, 0), iota(shape, 1)
    ours = (row >= copy * heads) & (row < (copy + 2) * heads) & (row % heads == lane // HEAD_DIM)
    return jnp.where(ours, 1.0, 0.0).astype(BF16)


def fill(table, parts):
    table[...] = jnp.zeros(table.shape, F32)
    count, _, lanes = table.shape
    for k, part in enumerate(parts):
        heads = part.shape[0] // count
        table[:, k * heads : (k + 1) * heads] = part.reshape(count, heads, lanes)


def silu_conv(scratch, block, taps):
    rows = block.shape[0] - HALO
    scratch[...] = block
    total = scratch[HALO - 3 : HALO - 3 + rows] * taps[0:1]
    for k in range(1, 4):
        total = total + scratch[HALO - 3 + k : HALO - 3 + k + rows] * taps[k : k + 1]
    return jax.nn.silu(total)


def turned(block):
    return pltpu.roll(block, HEAD_DIM, 1)


def pack_kernel(x_ref, coupling_ref, steps_ref, x_tail_ref, c_tail_ref, taps_ref, out_ref):
    count, _, lanes = out_ref.shape
    width = lanes - LANES
    rows = x_ref.shape[0]
    heads = steps_ref.shape[1] // count
    left = iota((HALO + rows, LANES), 1) < HEAD_DIM
    below = iota((HALO, width), 0) >= HALO - 3
    below_c = iota((HALO, LANES), 0) >= HALO - 3
    steps = steps_ref[...].astype(F32)
    steps = jnp.transpose(jnp.concatenate([steps, jnp.zeros((LANES - rows, steps.shape[1]), F32)], axis=0))
    own_taps = taps_ref[...].astype(F32)
    pair_width = GROUPS * STATE
    for d in range(count):
        g, j = d // 4, d % 4
        own = steps[d * heads : (d + 1) * heads]
        top = jnp.concatenate([own[:4], own[4:], jnp.zeros((4, width - 2 * LANES), F32)], axis=1)
        top = jnp.concatenate([top, jnp.zeros((HALO - 4, width), F32)], axis=0)
        lanes_d = slice(d * width, (d + 1) * width)
        top = jnp.where(below, x_tail_ref[:, lanes_d].astype(F32), top)
        out_ref[d, :, :width] = jnp.concatenate([top, x_ref[:, lanes_d].astype(F32)], axis=0).astype(BF16)
        taps = own_taps if j % 2 == 0 else turned(own_taps)
        taps = jnp.concatenate([taps, jnp.zeros((HALO - 4, LANES), F32)], axis=0)
        blocks = []
        for r in range(2):
            at = r * pair_width + g * STATE + j // 2 * LANES
            tail = c_tail_ref[:, at : at + LANES].astype(F32)
            blocks.append(jnp.concatenate([tail, coupling_ref[:, at : at + LANES].astype(F32)], axis=0))
        b, c = blocks
        both = jnp.where(left, b, turned(c)) if j % 2 == 0 else jnp.where(left, turned(b), c)
        both = jnp.concatenate([jnp.where(below_c, both[:HALO], taps), both[HALO:]], axis=0)
        out_ref[d, :, width:] = both.astype(BF16)


def coupling_kernel(from_ref, m_ref, b_ref, c_ref, steps_ref, scratch):
    count, _, lanes = m_ref.shape
    width = lanes - LANES
    rows = m_ref.shape[1] - HALO
    taps_b = m_ref[from_ref[0], :, width:].astype(F32)[:4]
    taps_c = turned(m_ref[from_ref[1], :, width:].astype(F32)[:4])
    taps = jnp.where(iota((4, LANES), 1) < HEAD_DIM, taps_b, taps_c)
    left = iota((rows // 2, LANES), 1) < HEAD_DIM

    def body(c, _):
        steps = m_ref[c, :, : 2 * LANES].astype(F32)
        steps_ref[c] = jnp.concatenate([steps[:4, :LANES], steps[:4, LANES:]], axis=0)
        both = silu_conv(scratch, m_ref[c, :, width:].astype(F32), taps)
        early, late = both[: rows // 2], both[rows // 2 :]
        b_ref[c] = jnp.where(left, early, turned(late)).astype(BF16)
        c_ref[c] = jnp.where(left, turned(early), late).astype(BF16)
        return 0

    lax.fori_loop(0, count, body, 0)


def unpacked(pieces):
    early, late = [], []
    for k in range(0, 4, 2):
        a, b = pieces[k].astype(F32), pieces[k + 1].astype(F32)
        left = iota(a.shape, 1) < HEAD_DIM
        early.append(jnp.where(left, a, turned(b)))
        late.append(jnp.where(left, turned(a), b))
    whole = jnp.concatenate([jnp.concatenate(early, axis=1), jnp.concatenate(late, axis=1)], axis=0)
    return whole.astype(BF16)


def input_kernel(m_ref, taps_ref, steps_ref, bias_ref, log_rate_ref, x_ref, weighted_ref, total_ref, scratch, table):
    count, rows, width = x_ref.shape
    heads = steps_ref.shape[1]
    dt, cum, tot = decay_tables(steps_ref, bias_ref, log_rate_ref, rows)
    size = (count * heads, count * heads)
    later_mat = jnp.where(
        (iota(size, 0) % heads == iota(size, 1) % heads) & (iota(size, 1) // heads > iota(size, 0) // heads), 1.0, 0.0
    ).astype(F32)
    later = jnp.dot(later_mat, cum, precision=exact, preferred_element_type=F32)[:, rows - 1 : rows]
    fill(table, high_low(jnp.exp(later + (tot - cum)) * dt))
    total_ref[...] = jnp.broadcast_to((tot[0:heads] + later[0:heads, 0:1])[None], total_ref.shape)
    taps = taps_ref[...].astype(F32)
    spread = spread_matrix(heads, width, 0)

    def body(c, _):
        x = silu_conv(scratch, m_ref[c, :, :width].astype(F32), taps).astype(BF16)
        x_ref[c] = x
        columns = jnp.transpose(table[c])[:rows].astype(BF16)
        scale = jnp.dot(columns, spread, preferred_element_type=F32)
        weighted_ref[c] = (x.astype(F32) * scale).astype(BF16)
        return 0

    lax.fori_loop(0, count, body, 0)


def state_kernel(p0, p1, p2, p3, weighted_ref, totals_ref, state_ref, in_ref, decay_ref):
    count, rows, width = weighted_ref.shape
    heads = totals_ref.shape[1]

    def body(c, _):
        in_ref[c] = unpacked([p[c] for p in (p0, p1, p2, p3)])
        return 0

    lax.fori_loop(0, count, body, 0)
    own = iota((heads, width), 0) == iota((heads, width), 1) // HEAD_DIM
    for s in range(totals_ref.shape[0]):
        logs = jnp.where(own, jnp.broadcast_to(totals_ref[s][:, :1], own.shape), 0.0)
        decay_ref[s : s + 1] = jnp.exp(jnp.sum(logs, axis=0, keepdims=True))
    state = lax.dot_general(
        in_ref[...].reshape(count * rows, STATE),
        weighted_ref[...].reshape(count * rows, width),
        (((0,), (0,)), ((), ())),
        preferred_element_type=F32,
    )
    state_ref[...] = state.reshape(state_ref.shape).astype(BF16)


def relay_kernel(state_ref, decay_ref, out_ref):
    carried = jnp.zeros(state_ref.shape[1:], F32)
    for s in range(state_ref.shape[0]):
        out_ref[s] = carried.astype(BF16)
        carried = decay_ref[s : s + 1] * carried + state_ref[s].astype(F32)


def scan_kernel(j_ref, x_ref, in_ref, c_ref, steps_ref, bias_ref, log_rate_ref, skip_ref,
                y_ref, out_ref, state, table, column_logs, row_logs):
    count, rows, width = x_ref.shape
    heads = steps_ref.shape[1]
    dt, cum, tot = decay_tables(steps_ref, bias_ref, log_rate_ref, rows)
    blocked = (count, heads, dt.shape[1])
    fill(table, high_low(jnp.exp(tot - cum) * dt) + high_low(jnp.exp(cum)))
    column_logs[...] = (cum * LOG2E).reshape(blocked)
    row_logs[...] = ((jnp.log(dt) - cum) * LOG2E).reshape(blocked)
    spread_in, spread_out = spread_matrix(heads, width, 0), spread_matrix(heads, width, 2)
    skip = skip_ref[...]
    state[...] = jnp.zeros(state.shape, F32)
    causal = iota((rows, rows), 0) >= iota((rows, rows), 1)
    left = iota((rows, LANES), 1) < HEAD_DIM
    order = [lax.bitwise_xor(j_ref[0], d) for d in range(4)]

    def body(c, _):
        q = unpacked([c_ref[k, c] for k in order])
        out_ref[c] = q
        b, x = in_ref[c], x_ref[c]
        meet = lax.dot_general(q, b, (((1,), (1,)), ((), ())), preferred_element_type=F32)
        meet = jnp.where(causal, meet, 0.0)
        columns = jnp.transpose(table[c])[:rows].astype(BF16)
        scale_in = jnp.dot(columns, spread_in, preferred_element_type=F32)
        scale_out = jnp.dot(columns, spread_out, preferred_element_type=F32)
        logs = jnp.transpose(column_logs[c])[:rows]
        rows_c = row_logs[c]
        carried = jnp.dot(q, state[...].astype(BF16), preferred_element_type=F32) * scale_out
        x32 = x.astype(F32)
        for pair in range(width // LANES):
            lanes = slice(pair * LANES, (pair + 1) * LANES)
            both = []
            for k in range(2):
                h = 2 * pair + k
                mix = jnp.exp2(logs[:, h : h + 1] + rows_c[h : h + 1, :rows]) * meet
                both.append(jnp.dot(mix.astype(BF16), x[:, lanes], preferred_element_type=F32))
            mixed = jnp.where(left, both[0], both[1])
            y_ref[c, :, lanes] = mixed + carried[:, lanes] + skip[:, lanes] * x32[:, lanes]
        state[...] = state[...] * scale_out[rows - 1 : rows] + lax.dot_general(
            b, (x32 * scale_in).astype(BF16), (((0,), (0,)), ((), ())), preferred_element_type=F32
        )
        return 0

    lax.fori_loop(0, count, body, 0)


def carry_kernel(y_ref, out_ref, incoming_ref, steps_ref, bias_ref, log_rate_ref, sum_ref, table):
    count, rows, width = y_ref.shape
    heads = steps_ref.shape[1]
    _, cum, tot = decay_tables(steps_ref, bias_ref, log_rate_ref, rows)
    size = (count * heads, count * heads)
    earlier_mat = jnp.where(
        (iota(size, 0) % heads == iota(size, 1) % heads) & (iota(size, 1) // heads < iota(size, 0) // heads), 1.0, 0.0
    ).astype(F32)
    earlier = jnp.dot(earlier_mat, cum, precision=exact, preferred_element_type=F32)[:, rows - 1 : rows]
    fill(table, high_low(jnp.exp(earlier + cum)))
    spread = spread_matrix(heads, width, 0)
    incoming = incoming_ref[...]

    def body(c, _):
        columns = jnp.transpose(table[c])[:rows].astype(BF16)
        scale = jnp.dot(columns, spread, preferred_element_type=F32)
        carried = jnp.dot(out_ref[c], incoming, preferred_element_type=F32)
        sum_ref[c] = (y_ref[c] + carried * scale).astype(BF16)
        return 0

    lax.fori_loop(0, count, body, 0)


def finish_kernel(*refs):
    parts, (gate_ref, gain_ref, out_ref, gated_ref) = refs[:-4], refs[-4:]
    blocks, rows, width = parts[0].shape
    total = jnp.zeros((rows, 1), F32)
    pieces = [(z, p) for z in range(blocks) for p in range(len(parts))]
    for i, (z, p) in enumerate(pieces):
        lanes = slice(i * width, (i + 1) * width)
        gated = parts[p][z].astype(F32) * jax.nn.silu(gate_ref[:, lanes].astype(F32))
        gated_ref[:, lanes] = gated
        total = total + jnp.sum(gated * gated, axis=1, keepdims=True)
    scale = lax.rsqrt(total / (len(pieces) * width) + 1e-05)
    for i in range(len(pieces)):
        lanes = slice(i * width, (i + 1) * width)
        out_ref[:, lanes] = (gated_ref[:, lanes] * scale * gain_ref[:, lanes].astype(F32)).astype(BF16)


def call(kernel, outs, scratch, args, cost=(0, 0), smem_first=False):
    specs = [pl.BlockSpec(memory_space=pltpu.VMEM)] * len(args)
    if smem_first:
        specs[0] = pl.BlockSpec(memory_space=pltpu.SMEM)
    return pl.pallas_call(
        kernel,
        out_shape=outs,
        in_specs=specs,
        out_specs=jax.tree.map(lambda _: pl.BlockSpec(memory_space=pltpu.VMEM), outs),
        scratch_shapes=scratch,
        compiler_params=params,
        cost_estimate=pl.CostEstimate(flops=cost[0], bytes_accessed=cost[1], transcendentals=0),
    )(*args)


def local(
    ssm_input,
    gate_input,
    coupling,
    step_input,
    conv_input,
    conv_coupling,
    step_bias,
    log_rate,
    skip_gain,
    norm_gain,
):
    rows, channels = ssm_input.shape
    ring = lax.axis_size("fsdp")
    seq = lax.axis_size("seq")
    heads = step_bias.shape[0]
    width = conv_input.shape[1]
    struct = jax.ShapeDtypeStruct
    place = lax.axis_index("fsdp").astype(jnp.int32)
    bias, rate = step_bias.reshape(heads, 1), log_rate.reshape(heads, 1)

    route = [(i, i + 1) for i in range(seq * ring - 1)]
    x_tail, c_tail = lax.ppermute((ssm_input[rows - HALO :], coupling[rows - HALO :]), ("seq", "fsdp"), route)
    message = call(
        pack_kernel,
        struct((ring, HALO + rows, width + LANES), BF16),
        [],
        (ssm_input, coupling, step_input, x_tail, c_tail, conv_coupling),
        (0, 4000000),
    )
    message = lax.all_to_all(message, "fsdp", 0, 0)

    senders = 2 * (place // 4) + place % 4 // 2 + jnp.array([0, 2 * GROUPS], jnp.int32)
    packed = struct((ring, rows // 2, LANES), BF16)
    own_in, own_out, steps = call(
        coupling_kernel,
        (packed, packed, struct((ring, heads, LANES), F32)),
        [pltpu.VMEM((HALO + rows, LANES), F32)],
        (senders, message),
        (4000000, 3000000),
        True,
    )
    pieces = [own_in] + [lax.ppermute(own_in, "fsdp", [(i, i ^ d) for i in range(ring)]) for d in range(1, 4)]
    blocks = (ring, rows, width)
    x, weighted, totals = call(
        input_kernel,
        (struct(blocks, BF16), struct(blocks, BF16), struct((seq, heads, LANES), F32)),
        [pltpu.VMEM((HALO + rows, width), F32), pltpu.VMEM((ring, LANES, LANES), F32)],
        (message, conv_input, steps, bias, rate),
        (20000000, 6000000),
    )
    totals = lax.all_to_all(totals, "seq", 0, 0)
    share = STATE // seq
    state, read_in, decay = call(
        state_kernel,
        (struct((seq, share, width), BF16), struct((ring, rows, STATE), BF16), struct((seq, width), F32)),
        [],
        (*pieces, weighted, totals),
        (400000000, 5000000),
    )
    fours = [[4 * g + j for j in range(4)] for g in range(ring // 4)]
    own_out, _ = lax.optimization_barrier((own_out, read_in))
    all_out = lax.all_gather(own_out, "fsdp", axis=0, axis_index_groups=fours)
    state = lax.all_to_all(state, "seq", 0, 0)
    incoming = call(relay_kernel, struct((seq, share, width), BF16), [], (state, decay), (1000000, 600000))
    incoming = lax.all_to_all(incoming, "seq", 0, 0).reshape(STATE, width)
    table = pltpu.VMEM((ring, heads, LANES), F32)
    y, read_out = call(
        scan_kernel,
        (struct(blocks, F32), struct((ring, rows, STATE), BF16)),
        [pltpu.VMEM((STATE, width), F32), pltpu.VMEM((ring, LANES, LANES), F32), table, table],
        ((place % 4).reshape(1), x, read_in, all_out, steps, bias, rate, jnp.repeat(skip_gain, HEAD_DIM).reshape(1, width)),
        (1600000000, 8000000),
        True,
    )
    y = call(
        carry_kernel,
        struct(blocks, BF16),
        [pltpu.VMEM((ring, LANES, LANES), F32)],
        (y, read_out, incoming, steps, bias, rate),
        (400000000, 6000000),
    )
    y = lax.all_to_all(y, "fsdp", 0, 0)

    group_width = channels // GROUPS
    return pl.pallas_call(
        finish_kernel,
        grid=(GROUPS,),
        out_shape=struct(ssm_input.shape, BF16),
        in_specs=[
            pl.BlockSpec((ring // GROUPS, rows, width), lambda g: (g, 0, 0)),
            pl.BlockSpec((rows, group_width), lambda g: (0, g)),
            pl.BlockSpec((1, group_width), lambda g: (0, g)),
        ],
        out_specs=pl.BlockSpec((rows, group_width), lambda g: (0, g)),
        scratch_shapes=[pltpu.VMEM((rows, group_width), F32)],
        compiler_params=params,
    )(y, gate_input, norm_gain.reshape(1, -1))


def solution(mesh):
    return jax.shard_map(
        local,
        mesh=mesh,
        in_specs=(
            P(("batch", "seq", "fsdp"), None),
            P(("batch", "seq", "fsdp"), None),
            P(("batch", "seq", "fsdp"), None),
            P(("batch", "seq", "fsdp"), None),
            P(None, "fsdp"),
            P(None, "fsdp"),
            P("fsdp"),
            P("fsdp"),
            P("fsdp"),
            P(),
        ),
        out_specs=P(("batch", "seq", "fsdp"), None),
        check_vma=False,
    )
```

```python
import jax
import jax.numpy as jnp
from jax import lax
from jax.experimental import pallas as pl
from jax.experimental.pallas import tpu as pltpu
from jax.sharding import PartitionSpec as P

HEAD_DIM = 64
STATE = 256
GROUPS = 4
LANES = 128
HALO = 8
LOG2E = 1.4426950408889634

F32 = jnp.float32
BF16 = jnp.bfloat16
exact = lax.Precision.HIGHEST
params = pltpu.CompilerParams(vmem_limit_bytes=48 * 2**20)
wide = pltpu.CompilerParams(vmem_limit_bytes=60 * 2**20)


def iota(shape, dim):
    return lax.broadcasted_iota(jnp.int32, shape, dim)


def decay_tables(steps_ref, bias_ref, log_rate_ref, rows):
    count, heads, lanes = steps_ref.shape
    dt = jax.nn.softplus(steps_ref[...] + bias_ref[...][None])
    log_decay = -jnp.exp(log_rate_ref[...])[None] * dt
    size = (lanes, lanes)
    upper = jnp.where(iota(size, 0) <= iota(size, 1), 1.0, 0.0).astype(F32)
    flat = log_decay.reshape(count * heads, lanes)
    cum = jnp.dot(flat, upper, precision=exact, preferred_element_type=F32)
    return dt.reshape(count * heads, lanes), cum, cum[:, rows - 1 : rows]


def sums_of_others(cum, rows, heads, later):
    size = (cum.shape[0], cum.shape[0])
    mine, other = iota(size, 0), iota(size, 1)
    beyond = other // heads > mine // heads if later else other // heads < mine // heads
    chosen = jnp.where((mine % heads == other % heads) & beyond, 1.0, 0.0).astype(F32)
    return jnp.dot(chosen, cum, precision=exact, preferred_element_type=F32)[:, rows - 1 : rows]


def high_low(table):
    high = table.astype(BF16).astype(F32)
    return high, table - high


def spread_matrix(heads, width, copy):
    shape = (LANES, width)
    row, lane = iota(shape, 0), iota(shape, 1)
    ours = (row >= copy * heads) & (row < (copy + 2) * heads) & (row % heads == lane // HEAD_DIM)
    return jnp.where(ours, 1.0, 0.0).astype(BF16)


def fill(table, parts):
    table[...] = jnp.zeros(table.shape, F32)
    count, _, lanes = table.shape
    for k, part in enumerate(parts):
        heads = part.shape[0] // count
        table[:, k * heads : (k + 1) * heads] = part.reshape(count, heads, lanes)


def silu_conv(scratch, block, taps):
    rows = block.shape[0] - HALO
    scratch[...] = block
    total = scratch[HALO - 3 : HALO - 3 + rows] * taps[0:1]
    for k in range(1, 4):
        total = total + scratch[HALO - 3 + k : HALO - 3 + k + rows] * taps[k : k + 1]
    return jax.nn.silu(total)


def turned(block):
    return pltpu.roll(block, HEAD_DIM, 1)


def pack_kernel(x_ref, b_ref, c_ref, steps_ref, x_tail_ref, b_tail_ref, c_tail_ref, taps_ref, out_ref, turned_steps):
    count, _, lanes = out_ref.shape
    width = lanes - LANES
    rows = x_ref.shape[0]
    g = pl.program_id(0)
    heads = steps_ref.shape[1] // GROUPS // count
    left = iota((HALO + rows, LANES), 1) < HEAD_DIM
    below = iota((HALO, width), 0) >= HALO - 3
    below_c = iota((HALO, LANES), 0) >= HALO - 3

    @pl.when(g == 0)
    def _():
        steps = steps_ref[...].astype(F32)
        turned_steps[...] = jnp.transpose(
            jnp.concatenate([steps, jnp.zeros((LANES - rows, steps.shape[1]), F32)], axis=0)
        )

    own_taps = taps_ref[...].astype(F32)
    for j in range(count):
        own = turned_steps[pl.ds(pl.multiple_of((g * count + j) * heads, heads), heads)]
        top = jnp.concatenate([own[:4], own[4:], jnp.zeros((4, width - 2 * LANES), F32)], axis=1)
        top = jnp.concatenate([top, jnp.zeros((HALO - 4, width), F32)], axis=0)
        lanes_j = slice(j * width, (j + 1) * width)
        top = jnp.where(below, x_tail_ref[:, lanes_j].astype(F32), top)
        out_ref[j, :, :width] = jnp.concatenate([top, x_ref[:, lanes_j].astype(F32)], axis=0).astype(BF16)
        taps = own_taps if j % 2 == 0 else turned(own_taps)
        taps = jnp.concatenate([taps, jnp.zeros((HALO - 4, LANES), F32)], axis=0)
        half = slice(j // 2 * LANES, (j // 2 + 1) * LANES)
        b = jnp.concatenate([b_tail_ref[:, half].astype(F32), b_ref[:, half].astype(F32)], axis=0)
        c = jnp.concatenate([c_tail_ref[:, half].astype(F32), c_ref[:, half].astype(F32)], axis=0)
        both = jnp.where(left, b, turned(c)) if j % 2 == 0 else jnp.where(left, turned(b), c)
        both = jnp.concatenate([jnp.where(below_c, both[:HALO], taps), both[HALO:]], axis=0)
        out_ref[j, :, width:] = both.astype(BF16)


def coupling_kernel(from_ref, m_ref, b_ref, c_ref, steps_ref, scratch):
    count, _, lanes = m_ref.shape
    width = lanes - LANES
    rows = m_ref.shape[1] - HALO
    taps_b = m_ref[from_ref[0], :, width:].astype(F32)[:4]
    taps_c = turned(m_ref[from_ref[1], :, width:].astype(F32)[:4])
    taps = jnp.where(iota((4, LANES), 1) < HEAD_DIM, taps_b, taps_c)
    left = iota((rows // 2, LANES), 1) < HEAD_DIM

    def body(c, _):
        steps = m_ref[c, :, : 2 * LANES].astype(F32)
        steps_ref[c] = jnp.concatenate([steps[:4, :LANES], steps[:4, LANES:]], axis=0)
        both = silu_conv(scratch, m_ref[c, :, width:].astype(F32), taps)
        early, late = both[: rows // 2], both[rows // 2 :]
        b_ref[c] = jnp.where(left, early, turned(late)).astype(BF16)
        c_ref[c] = jnp.where(left, turned(early), late).astype(BF16)
        return 0

    lax.fori_loop(0, count, body, 0)


def unpacked(pieces):
    early, late = [], []
    for k in range(0, 4, 2):
        a, b = pieces[k].astype(F32), pieces[k + 1].astype(F32)
        left = iota(a.shape, 1) < HEAD_DIM
        early.append(jnp.where(left, a, turned(b)))
        late.append(jnp.where(left, turned(a), b))
    whole = jnp.concatenate([jnp.concatenate(early, axis=1), jnp.concatenate(late, axis=1)], axis=0)
    return whole.astype(BF16)


def input_kernel(m_ref, taps_ref, steps_ref, bias_ref, log_rate_ref, x_ref, weighted_ref, total_ref, scratch, table):
    count, rows, width = x_ref.shape
    heads = steps_ref.shape[1]
    dt, cum, tot = decay_tables(steps_ref, bias_ref, log_rate_ref, rows)
    later = sums_of_others(cum, rows, heads, True)
    fill(table, high_low(jnp.exp(later + (tot - cum)) * dt))
    own = iota((heads, width), 0) == iota((heads, width), 1) // HEAD_DIM
    section = jnp.broadcast_to(tot[0:heads] + later[0:heads, 0:1], own.shape)
    logs = jnp.sum(jnp.where(own, section, 0.0), axis=0, keepdims=True)
    total_ref[...] = jnp.broadcast_to(logs, total_ref.shape)
    taps = taps_ref[...].astype(F32)
    spread = spread_matrix(heads, width, 0)

    def body(c, _):
        x = silu_conv(scratch, m_ref[c, :, :width].astype(F32), taps).astype(BF16)
        x_ref[c] = x
        columns = jnp.transpose(table[c])[:rows].astype(BF16)
        scale = jnp.dot(columns, spread, preferred_element_type=F32)
        weighted_ref[c] = (x.astype(F32) * scale).astype(BF16)
        return 0

    lax.fori_loop(0, count, body, 0)


def state_kernel(p0, p1, p2, p3, weighted_ref, logs_ref, state_ref, in_ref):
    count, rows, width = weighted_ref.shape
    sections, share_rows, _ = state_ref.shape

    def body(c, _):
        in_ref[c] = unpacked([p[c] for p in (p0, p1, p2, p3)])
        return 0

    lax.fori_loop(0, count, body, 0, unroll=4)
    state = lax.dot_general(
        in_ref[...].reshape(count * rows, STATE),
        weighted_ref[...].reshape(count * rows, width),
        (((0,), (0,)), ((), ())),
        preferred_element_type=F32,
    )
    high, low = high_low(logs_ref[...])
    logs = jnp.where(iota(high.shape, 0) == 0, high, low)
    share = STATE // sections
    for s in range(sections):
        block = jnp.concatenate([state[s * share : (s + 1) * share], logs], axis=0)
        state_ref[s] = block.astype(BF16)


def relay_kernel(state_ref, out_ref):
    share = out_ref.shape[1]
    carried = jnp.zeros(out_ref.shape[1:], F32)
    for s in range(state_ref.shape[0]):
        out_ref[s] = carried.astype(BF16)
        block = state_ref[s].astype(F32)
        decay = jnp.exp(block[share : share + 1] + block[share + 1 : share + 2])
        carried = decay * carried + block[:share]


def scan_kernel(x_ref, in_ref, p0, p1, p2, p3, steps_ref, bias_ref, log_rate_ref, skip_ref,
                y_ref, out_ref, scale_ref, state, table, column_logs, row_logs):
    count, rows, width = x_ref.shape
    heads = steps_ref.shape[1]
    dt, cum, tot = decay_tables(steps_ref, bias_ref, log_rate_ref, rows)
    blocked = (count, heads, dt.shape[1])
    earlier = sums_of_others(cum, rows, heads, False)
    fill(table, high_low(jnp.exp(tot - cum) * dt) + high_low(jnp.exp(cum)) + high_low(jnp.exp(earlier + cum)))
    column_logs[...] = (cum * LOG2E).reshape(blocked)
    row_logs[...] = ((jnp.log(dt) - cum) * LOG2E).reshape(blocked)
    spread_in, spread_out, spread_all = (spread_matrix(heads, width, k) for k in (0, 2, 4))
    skip = skip_ref[...]
    state[...] = jnp.zeros(state.shape, F32)
    causal = iota((rows, rows), 0) >= iota((rows, rows), 1)
    left = iota((rows, LANES), 1) < HEAD_DIM

    def body(c, _):
        q = unpacked([p[c] for p in (p0, p1, p2, p3)])
        out_ref[c] = q
        b, x = in_ref[c], x_ref[c]
        meet = lax.dot_general(q, b, (((1,), (1,)), ((), ())), preferred_element_type=F32)
        meet = jnp.where(causal, meet, 0.0)
        columns = jnp.transpose(table[c])[:rows].astype(BF16)
        scale_in = jnp.dot(columns, spread_in, preferred_element_type=F32)
        scale_out = jnp.dot(columns, spread_out, preferred_element_type=F32)
        scale_ref[c] = jnp.dot(columns, spread_all, preferred_element_type=F32)
        logs = jnp.transpose(column_logs[c])[:rows]
        rows_c = row_logs[c]
        carried = jnp.dot(q, state[...].astype(BF16), preferred_element_type=F32) * scale_out
        x32 = x.astype(F32)
        for pair in range(width // LANES):
            lanes = slice(pair * LANES, (pair + 1) * LANES)
            both = []
            for k in range(2):
                h = 2 * pair + k
                mix = jnp.exp2(logs[:, h : h + 1] + rows_c[h : h + 1, :rows]) * meet
                both.append(jnp.dot(mix.astype(BF16), x[:, lanes], preferred_element_type=F32))
            mixed = jnp.where(left, both[0], both[1])
            y_ref[c, :, lanes] = mixed + carried[:, lanes] + skip[:, lanes] * x32[:, lanes]
        state[...] = state[...] * scale_out[rows - 1 : rows] + lax.dot_general(
            b, (x32 * scale_in).astype(BF16), (((0,), (0,)), ((), ())), preferred_element_type=F32
        )
        return 0

    lax.fori_loop(0, count, body, 0)


def carry_kernel(y_ref, out_ref, scale_ref, incoming_ref, sum_ref):
    incoming = incoming_ref[...]

    def body(c, _):
        carried = jnp.dot(out_ref[c], incoming, preferred_element_type=F32)
        sum_ref[c] = (y_ref[c] + carried * scale_ref[c]).astype(BF16)
        return 0

    lax.fori_loop(0, y_ref.shape[0], body, 0, unroll=4)


def finish_kernel(*refs):
    parts, (gate_ref, gain_ref, out_ref, gated_ref) = refs[:-4], refs[-4:]
    blocks, rows, width = parts[0].shape
    total = jnp.zeros((rows, 1), F32)
    pieces = [(z, p) for z in range(blocks) for p in range(len(parts))]
    for i, (z, p) in enumerate(pieces):
        lanes = slice(i * width, (i + 1) * width)
        gated = parts[p][z].astype(F32) * jax.nn.silu(gate_ref[:, lanes].astype(F32))
        gated_ref[:, lanes] = gated
        total = total + jnp.sum(gated * gated, axis=1, keepdims=True)
    scale = lax.rsqrt(total / (len(pieces) * width) + 1e-05)
    for i in range(len(pieces)):
        lanes = slice(i * width, (i + 1) * width)
        out_ref[:, lanes] = (gated_ref[:, lanes] * scale * gain_ref[:, lanes].astype(F32)).astype(BF16)


def call(kernel, outs, scratch, args, cost=(0, 0), smem_first=False):
    specs = [pl.BlockSpec(memory_space=pltpu.VMEM)] * len(args)
    if smem_first:
        specs[0] = pl.BlockSpec(memory_space=pltpu.SMEM)
    return pl.pallas_call(
        kernel,
        out_shape=outs,
        in_specs=specs,
        out_specs=jax.tree.map(lambda _: pl.BlockSpec(memory_space=pltpu.VMEM), outs),
        scratch_shapes=scratch,
        compiler_params=params,
        cost_estimate=pl.CostEstimate(flops=cost[0], bytes_accessed=cost[1], transcendentals=0),
    )(*args)


def local(
    ssm_input,
    gate_input,
    coupling,
    step_input,
    conv_input,
    conv_coupling,
    step_bias,
    log_rate,
    skip_gain,
    norm_gain,
):
    rows, channels = ssm_input.shape
    ring = lax.axis_size("fsdp")
    seq = lax.axis_size("seq")
    heads = step_bias.shape[0]
    width = conv_input.shape[1]
    struct = jax.ShapeDtypeStruct
    place = lax.axis_index("fsdp").astype(jnp.int32)
    bias, rate = step_bias.reshape(heads, 1), log_rate.reshape(heads, 1)

    route = [(i, i + 1) for i in range(seq * ring - 1)]
    x_tail, c_tail = lax.ppermute((ssm_input[rows - HALO :], coupling[rows - HALO :]), ("seq", "fsdp"), route)
    group_width = channels // GROUPS

    def columns_of(count, size, first):
        return pl.BlockSpec((count, size), lambda g: (0, first + g))

    def same(*shape):
        return pl.BlockSpec(shape, lambda g: (0,) * len(shape))

    message = pl.pallas_call(
        pack_kernel,
        grid=(GROUPS,),
        out_shape=struct((ring, HALO + rows, width + LANES), BF16),
        in_specs=[
            columns_of(rows, group_width, 0),
            columns_of(rows, STATE, 0),
            columns_of(rows, STATE, GROUPS),
            same(*step_input.shape),
            columns_of(HALO, group_width, 0),
            columns_of(HALO, STATE, 0),
            columns_of(HALO, STATE, GROUPS),
            same(*conv_coupling.shape),
        ],
        out_specs=pl.BlockSpec((ring // GROUPS, HALO + rows, width + LANES), lambda g: (g, 0, 0)),
        scratch_shapes=[pltpu.VMEM((LANES, LANES), F32)],
        compiler_params=wide,
    )(ssm_input, coupling, coupling, step_input, x_tail, c_tail, c_tail, conv_coupling)
    message = lax.all_to_all(message, "fsdp", 0, 0)

    senders = 2 * (place // 4) + place % 4 // 2 + jnp.array([0, 2 * GROUPS], jnp.int32)
    packed = struct((ring, rows // 2, LANES), BF16)
    own_in, own_out, steps = call(
        coupling_kernel,
        (packed, packed, struct((ring, heads, LANES), F32)),
        [pltpu.VMEM((HALO + rows, LANES), F32)],
        (senders, message),
        (4000000, 3000000),
        True,
    )
    pieces = [own_in] + [lax.ppermute(own_in, "fsdp", [(i, i ^ d) for i in range(ring)]) for d in range(1, 4)]
    blocks = (ring, rows, width)
    x, weighted, logs = call(
        input_kernel,
        (struct(blocks, BF16), struct(blocks, BF16), struct((8, width), F32)),
        [pltpu.VMEM((HALO + rows, width), F32), pltpu.VMEM((ring, LANES, LANES), F32)],
        (message, conv_input, steps, bias, rate),
        (6000000000, 6000000),
    )
    own_out, weighted = lax.optimization_barrier((own_out, weighted))
    out_pieces = [own_out] + [lax.ppermute(own_out, "fsdp", [(i, i ^ d) for i in range(ring)]) for d in range(1, 4)]
    share = STATE // seq
    state, read_in = call(
        state_kernel,
        (struct((seq, share + 8, width), BF16), struct((ring, rows, STATE), BF16)),
        [],
        (*pieces, weighted, logs),
        (2000000000, 5000000),
    )
    state = lax.all_to_all(state, "seq", 0, 0)
    incoming = call(relay_kernel, struct((seq, share, width), BF16), [], (state,), (500000000, 600000))
    incoming = lax.all_to_all(incoming, "seq", 0, 0).reshape(STATE, width)
    table = pltpu.VMEM((ring, heads, LANES), F32)
    y, read_out, scale = call(
        scan_kernel,
        (struct(blocks, F32), struct((ring, rows, STATE), BF16), struct(blocks, F32)),
        [pltpu.VMEM((STATE, width), F32), pltpu.VMEM((ring, LANES, LANES), F32), table, table],
        (x, read_in, *out_pieces, steps, bias, rate, jnp.repeat(skip_gain, HEAD_DIM).reshape(1, width)),
        (10000000000, 8000000),
    )
    y = call(carry_kernel, struct(blocks, BF16), [], (y, read_out, scale, incoming), (3000000000, 6000000))
    y = lax.all_to_all(y, "fsdp", 0, 0)

    return pl.pallas_call(
        finish_kernel,
        grid=(GROUPS,),
        out_shape=struct(ssm_input.shape, BF16),
        in_specs=[
            pl.BlockSpec((ring // GROUPS, rows, width), lambda g: (g, 0, 0)),
            pl.BlockSpec((rows, group_width), lambda g: (0, g)),
            pl.BlockSpec((1, group_width), lambda g: (0, g)),
        ],
        out_specs=pl.BlockSpec((rows, group_width), lambda g: (0, g)),
        scratch_shapes=[pltpu.VMEM((rows, group_width), F32)],
        compiler_params=wide,
    )(y, gate_input, norm_gain.reshape(1, -1))


def solution(mesh):
    return jax.shard_map(
        local,
        mesh=mesh,
        in_specs=(
            P(("batch", "seq", "fsdp"), None),
            P(("batch", "seq", "fsdp"), None),
            P(("batch", "seq", "fsdp"), None),
            P(("batch", "seq", "fsdp"), None),
            P(None, "fsdp"),
            P(None, "fsdp"),
            P("fsdp"),
            P("fsdp"),
            P("fsdp"),
            P(),
        ),
        out_specs=P(("batch", "seq", "fsdp"), None),
        check_vma=False,
    )
```

```python
import jax
import jax.numpy as jnp
from jax import lax
from jax.experimental import pallas as pl
from jax.experimental.pallas import tpu as pltpu
from jax.sharding import PartitionSpec as P

HEAD_DIM = 64
STATE = 256
GROUPS = 4
LANES = 128
HALO = 8
LOG2E = 1.4426950408889634

F32 = jnp.float32
BF16 = jnp.bfloat16
exact = lax.Precision.HIGHEST
params = pltpu.CompilerParams(vmem_limit_bytes=48 * 2**20)
wide = pltpu.CompilerParams(vmem_limit_bytes=60 * 2**20)


def iota(shape, dim):
    return lax.broadcasted_iota(jnp.int32, shape, dim)


def decay_tables(steps_ref, bias_ref, log_rate_ref, rows):
    count, heads, lanes = steps_ref.shape
    dt = jax.nn.softplus(steps_ref[...] + bias_ref[...][None])
    log_decay = -jnp.exp(log_rate_ref[...])[None] * dt
    size = (lanes, lanes)
    upper = jnp.where(iota(size, 0) <= iota(size, 1), 1.0, 0.0).astype(F32)
    flat = log_decay.reshape(count * heads, lanes)
    cum = jnp.dot(flat, upper, precision=exact, preferred_element_type=F32)
    return dt.reshape(count * heads, lanes), cum, cum[:, rows - 1 : rows]


def sums_of_others(cum, rows, heads, later):
    size = (cum.shape[0], cum.shape[0])
    mine, other = iota(size, 0), iota(size, 1)
    beyond = other // heads > mine // heads if later else other // heads < mine // heads
    chosen = jnp.where((mine % heads == other % heads) & beyond, 1.0, 0.0).astype(F32)
    return jnp.dot(chosen, cum, precision=exact, preferred_element_type=F32)[:, rows - 1 : rows]


def high_low(table):
    high = table.astype(BF16).astype(F32)
    return high, table - high


def spread_matrix(heads, width, copy):
    shape = (LANES, width)
    row, lane = iota(shape, 0), iota(shape, 1)
    ours = (row >= copy * heads) & (row < (copy + 2) * heads) & (row % heads == lane // HEAD_DIM)
    return jnp.where(ours, 1.0, 0.0).astype(BF16)


def fill(table, parts):
    table[...] = jnp.zeros(table.shape, F32)
    count, _, lanes = table.shape
    for k, part in enumerate(parts):
        heads = part.shape[0] // count
        table[:, k * heads : (k + 1) * heads] = part.reshape(count, heads, lanes)


def silu_conv(scratch, block, taps):
    rows = block.shape[0] - HALO
    scratch[...] = block
    total = scratch[HALO - 3 : HALO - 3 + rows] * taps[0:1]
    for k in range(1, 4):
        total = total + scratch[HALO - 3 + k : HALO - 3 + k + rows] * taps[k : k + 1]
    return jax.nn.silu(total)


def turned(block):
    return pltpu.roll(block, HEAD_DIM, 1)


def pack_kernel(x_ref, b_ref, c_ref, steps_ref, x_tail_ref, b_tail_ref, c_tail_ref, taps_ref, out_ref, turned_steps):
    count, _, lanes = out_ref.shape
    width = lanes - LANES
    rows = x_ref.shape[0]
    g = pl.program_id(0)
    heads = steps_ref.shape[1] // GROUPS // count
    left = iota((HALO + rows, LANES), 1) < HEAD_DIM
    below = iota((HALO, width), 0) >= HALO - 3
    below_c = iota((HALO, LANES), 0) >= HALO - 3

    @pl.when(g == 0)
    def _():
        steps = steps_ref[...].astype(F32)
        turned_steps[...] = jnp.transpose(
            jnp.concatenate([steps, jnp.zeros((LANES - rows, steps.shape[1]), F32)], axis=0)
        )

    own_taps = taps_ref[...].astype(F32)
    for j in range(count):
        own = turned_steps[pl.ds(pl.multiple_of((g * count + j) * heads, heads), heads)]
        top = jnp.concatenate([own[:4], own[4:], jnp.zeros((4, width - 2 * LANES), F32)], axis=1)
        top = jnp.concatenate([top, jnp.zeros((HALO - 4, width), F32)], axis=0)
        lanes_j = slice(j * width, (j + 1) * width)
        top = jnp.where(below, x_tail_ref[:, lanes_j].astype(F32), top)
        out_ref[j, :, :width] = jnp.concatenate([top, x_ref[:, lanes_j].astype(F32)], axis=0).astype(BF16)
        taps = own_taps if j % 2 == 0 else turned(own_taps)
        taps = jnp.concatenate([taps, jnp.zeros((HALO - 4, LANES), F32)], axis=0)
        half = slice(j // 2 * LANES, (j // 2 + 1) * LANES)
        b = jnp.concatenate([b_tail_ref[:, half].astype(F32), b_ref[:, half].astype(F32)], axis=0)
        c = jnp.concatenate([c_tail_ref[:, half].astype(F32), c_ref[:, half].astype(F32)], axis=0)
        both = jnp.where(left, b, turned(c)) if j % 2 == 0 else jnp.where(left, turned(b), c)
        both = jnp.concatenate([jnp.where(below_c, both[:HALO], taps), both[HALO:]], axis=0)
        out_ref[j, :, width:] = both.astype(BF16)


def coupling_kernel(from_ref, m_ref, b_ref, c_ref, steps_ref, scratch):
    count, _, lanes = m_ref.shape
    width = lanes - LANES
    rows = m_ref.shape[1] - HALO
    taps_b = m_ref[from_ref[0], :, width:].astype(F32)[:4]
    taps_c = turned(m_ref[from_ref[1], :, width:].astype(F32)[:4])
    taps = jnp.where(iota((4, LANES), 1) < HEAD_DIM, taps_b, taps_c)
    left = iota((rows // 2, LANES), 1) < HEAD_DIM

    def body(c, _):
        steps = m_ref[c, :, : 2 * LANES].astype(F32)
        steps_ref[c] = jnp.concatenate([steps[:4, :LANES], steps[:4, LANES:]], axis=0)
        both = silu_conv(scratch, m_ref[c, :, width:].astype(F32), taps)
        early, late = both[: rows // 2], both[rows // 2 :]
        b_ref[c] = jnp.where(left, early, turned(late)).astype(BF16)
        c_ref[c] = jnp.where(left, turned(early), late).astype(BF16)
        return 0

    lax.fori_loop(0, count, body, 0, unroll=4)


def unpacked(pieces):
    early, late = [], []
    for k in range(0, 4, 2):
        a, b = pieces[k].astype(F32), pieces[k + 1].astype(F32)
        left = iota(a.shape, 1) < HEAD_DIM
        early.append(jnp.where(left, a, turned(b)))
        late.append(jnp.where(left, turned(a), b))
    whole = jnp.concatenate([jnp.concatenate(early, axis=1), jnp.concatenate(late, axis=1)], axis=0)
    return whole.astype(BF16)


def input_kernel(m_ref, taps_ref, steps_ref, bias_ref, log_rate_ref, x_ref, weighted_ref, total_ref, scratch, table):
    count, rows, width = x_ref.shape
    heads = steps_ref.shape[1]
    dt, cum, tot = decay_tables(steps_ref, bias_ref, log_rate_ref, rows)
    later = sums_of_others(cum, rows, heads, True)
    fill(table, high_low(jnp.exp(later + (tot - cum)) * dt))
    own = iota((heads, width), 0) == iota((heads, width), 1) // HEAD_DIM
    section = jnp.broadcast_to(tot[0:heads] + later[0:heads, 0:1], own.shape)
    logs = jnp.sum(jnp.where(own, section, 0.0), axis=0, keepdims=True)
    total_ref[...] = jnp.broadcast_to(logs, total_ref.shape)
    taps = taps_ref[...].astype(F32)
    spread = spread_matrix(heads, width, 0)

    def body(c, _):
        x = silu_conv(scratch, m_ref[c, :, :width].astype(F32), taps).astype(BF16)
        x_ref[c] = x
        columns = jnp.transpose(table[c])[:rows].astype(BF16)
        scale = jnp.dot(columns, spread, preferred_element_type=F32)
        weighted_ref[c] = (x.astype(F32) * scale).astype(BF16)
        return 0

    lax.fori_loop(0, count, body, 0, unroll=4)


def state_kernel(p0, p1, p2, p3, weighted_ref, logs_ref, state_ref, in_ref):
    count, rows, width = weighted_ref.shape
    sections, share_rows, _ = state_ref.shape

    def body(c, _):
        in_ref[c] = unpacked([p[c] for p in (p0, p1, p2, p3)])
        return 0

    lax.fori_loop(0, count, body, 0, unroll=4)
    state = lax.dot_general(
        in_ref[...].reshape(count * rows, STATE),
        weighted_ref[...].reshape(count * rows, width),
        (((0,), (0,)), ((), ())),
        preferred_element_type=F32,
    )
    high, low = high_low(logs_ref[...])
    logs = jnp.where(iota(high.shape, 0) == 0, high, low)
    share = STATE // sections
    for s in range(sections):
        block = jnp.concatenate([state[s * share : (s + 1) * share], logs], axis=0)
        state_ref[s] = block.astype(BF16)


def relay_kernel(state_ref, out_ref):
    share = out_ref.shape[1]
    carried = jnp.zeros(out_ref.shape[1:], F32)
    for s in range(state_ref.shape[0]):
        out_ref[s] = carried.astype(BF16)
        block = state_ref[s].astype(F32)
        decay = jnp.exp(block[share : share + 1] + block[share + 1 : share + 2])
        carried = decay * carried + block[:share]


def scan_kernel(x_ref, in_ref, p0, p1, p2, p3, steps_ref, bias_ref, log_rate_ref, skip_ref,
                y_ref, out_ref, scale_ref, state, table, column_logs, row_logs):
    count, rows, width = x_ref.shape
    heads = steps_ref.shape[1]
    dt, cum, tot = decay_tables(steps_ref, bias_ref, log_rate_ref, rows)
    blocked = (count, heads, dt.shape[1])
    earlier = sums_of_others(cum, rows, heads, False)
    fill(table, high_low(jnp.exp(tot - cum) * dt) + high_low(jnp.exp(cum)) + high_low(jnp.exp(earlier + cum)))
    column_logs[...] = (cum * LOG2E).reshape(blocked)
    row_logs[...] = ((jnp.log(dt) - cum) * LOG2E).reshape(blocked)
    spread_in, spread_out, spread_all = (spread_matrix(heads, width, k) for k in (0, 2, 4))
    skip = skip_ref[...]
    state[...] = jnp.zeros(state.shape, F32)
    causal = iota((rows, rows), 0) >= iota((rows, rows), 1)
    left = iota((rows, LANES), 1) < HEAD_DIM

    def body(c, _):
        q = unpacked([p[c] for p in (p0, p1, p2, p3)])
        out_ref[c] = q
        b, x = in_ref[c], x_ref[c]
        meet = lax.dot_general(q, b, (((1,), (1,)), ((), ())), preferred_element_type=F32)
        meet = jnp.where(causal, meet, 0.0)
        columns = jnp.transpose(table[c])[:rows].astype(BF16)
        scale_in = jnp.dot(columns, spread_in, preferred_element_type=F32)
        scale_out = jnp.dot(columns, spread_out, preferred_element_type=F32)
        scale_ref[c] = jnp.dot(columns, spread_all, preferred_element_type=F32)
        logs = jnp.transpose(column_logs[c])[:rows]
        rows_c = row_logs[c]
        carried = jnp.dot(q, state[...].astype(BF16), preferred_element_type=F32) * scale_out
        x32 = x.astype(F32)
        for pair in range(width // LANES):
            lanes = slice(pair * LANES, (pair + 1) * LANES)
            both = []
            for k in range(2):
                h = 2 * pair + k
                mix = jnp.exp2(logs[:, h : h + 1] + rows_c[h : h + 1, :rows]) * meet
                both.append(jnp.dot(mix.astype(BF16), x[:, lanes], preferred_element_type=F32))
            mixed = jnp.where(left, both[0], both[1])
            y_ref[c, :, lanes] = mixed + carried[:, lanes] + skip[:, lanes] * x32[:, lanes]
        state[...] = state[...] * scale_out[rows - 1 : rows] + lax.dot_general(
            b, (x32 * scale_in).astype(BF16), (((0,), (0,)), ((), ())), preferred_element_type=F32
        )
        return 0

    lax.fori_loop(0, count, body, 0, unroll=4)


def carry_kernel(y_ref, out_ref, scale_ref, incoming_ref, sum_ref):
    incoming = incoming_ref[...]

    def body(c, _):
        carried = jnp.dot(out_ref[c], incoming, preferred_element_type=F32)
        sum_ref[c] = (y_ref[c] + carried * scale_ref[c]).astype(BF16)
        return 0

    lax.fori_loop(0, y_ref.shape[0], body, 0, unroll=4)


def finish_kernel(*refs):
    parts, (gate_ref, gain_ref, out_ref, gated_ref) = refs[:-4], refs[-4:]
    blocks, rows, width = parts[0].shape
    total = jnp.zeros((rows, 1), F32)
    pieces = [(z, p) for z in range(blocks) for p in range(len(parts))]
    for i, (z, p) in enumerate(pieces):
        lanes = slice(i * width, (i + 1) * width)
        gated = parts[p][z].astype(F32) * jax.nn.silu(gate_ref[:, lanes].astype(F32))
        gated_ref[:, lanes] = gated
        total = total + jnp.sum(gated * gated, axis=1, keepdims=True)
    scale = lax.rsqrt(total / (len(pieces) * width) + 1e-05)
    for i in range(len(pieces)):
        lanes = slice(i * width, (i + 1) * width)
        out_ref[:, lanes] = (gated_ref[:, lanes] * scale * gain_ref[:, lanes].astype(F32)).astype(BF16)


def call(kernel, outs, scratch, args, cost=(0, 0), smem_first=False):
    specs = [pl.BlockSpec(memory_space=pltpu.VMEM)] * len(args)
    if smem_first:
        specs[0] = pl.BlockSpec(memory_space=pltpu.SMEM)
    return pl.pallas_call(
        kernel,
        out_shape=outs,
        in_specs=specs,
        out_specs=jax.tree.map(lambda _: pl.BlockSpec(memory_space=pltpu.VMEM), outs),
        scratch_shapes=scratch,
        compiler_params=params,
        cost_estimate=pl.CostEstimate(flops=cost[0], bytes_accessed=cost[1], transcendentals=0),
    )(*args)


def local(
    ssm_input,
    gate_input,
    coupling,
    step_input,
    conv_input,
    conv_coupling,
    step_bias,
    log_rate,
    skip_gain,
    norm_gain,
):
    rows, channels = ssm_input.shape
    ring = lax.axis_size("fsdp")
    seq = lax.axis_size("seq")
    heads = step_bias.shape[0]
    width = conv_input.shape[1]
    struct = jax.ShapeDtypeStruct
    place = lax.axis_index("fsdp").astype(jnp.int32)
    bias, rate = step_bias.reshape(heads, 1), log_rate.reshape(heads, 1)

    route = [(i, i + 1) for i in range(seq * ring - 1)]
    last_rows = jnp.concatenate([ssm_input[rows - HALO :], coupling[rows - HALO :]], axis=1)
    tails = lax.ppermute(last_rows, ("seq", "fsdp"), route)
    group_width = channels // GROUPS

    def columns_of(count, size, first):
        return pl.BlockSpec((count, size), lambda g: (0, first + g))

    def same(*shape):
        return pl.BlockSpec(shape, lambda g: (0,) * len(shape))

    message = pl.pallas_call(
        pack_kernel,
        grid=(GROUPS,),
        out_shape=struct((ring, HALO + rows, width + LANES), BF16),
        in_specs=[
            columns_of(rows, group_width, 0),
            columns_of(rows, STATE, 0),
            columns_of(rows, STATE, GROUPS),
            same(*step_input.shape),
            columns_of(HALO, group_width, 0),
            columns_of(HALO, STATE, channels // STATE),
            columns_of(HALO, STATE, channels // STATE + GROUPS),
            same(*conv_coupling.shape),
        ],
        out_specs=pl.BlockSpec((ring // GROUPS, HALO + rows, width + LANES), lambda g: (g, 0, 0)),
        scratch_shapes=[pltpu.VMEM((LANES, LANES), F32)],
        compiler_params=wide,
    )(ssm_input, coupling, coupling, step_input, tails, tails, tails, conv_coupling)
    message = lax.all_to_all(message, "fsdp", 0, 0)

    senders = 2 * (place // 4) + place % 4 // 2 + jnp.array([0, 2 * GROUPS], jnp.int32)
    packed = struct((ring, rows // 2, LANES), BF16)
    own_in, own_out, steps = call(
        coupling_kernel,
        (packed, packed, struct((ring, heads, LANES), F32)),
        [pltpu.VMEM((HALO + rows, LANES), F32)],
        (senders, message),
        (4000000, 3000000),
        True,
    )
    pieces = [own_in] + [lax.ppermute(own_in, "fsdp", [(i, i ^ d) for i in range(ring)]) for d in range(1, 4)]
    blocks = (ring, rows, width)
    x, weighted, logs = call(
        input_kernel,
        (struct(blocks, BF16), struct(blocks, BF16), struct((8, width), F32)),
        [pltpu.VMEM((HALO + rows, width), F32), pltpu.VMEM((ring, LANES, LANES), F32)],
        (message, conv_input, steps, bias, rate),
        (6000000000, 6000000),
    )
    own_out, weighted = lax.optimization_barrier((own_out, weighted))
    out_pieces = [own_out] + [lax.ppermute(own_out, "fsdp", [(i, i ^ d) for i in range(ring)]) for d in range(1, 4)]
    share = STATE // seq
    state, read_in = call(
        state_kernel,
        (struct((seq, share + 8, width), BF16), struct((ring, rows, STATE), BF16)),
        [],
        (*pieces, weighted, logs),
        (2000000000, 5000000),
    )
    state = lax.all_to_all(state, "seq", 0, 0)
    incoming = call(relay_kernel, struct((seq, share, width), BF16), [], (state,), (500000000, 600000))
    incoming = lax.all_to_all(incoming, "seq", 0, 0).reshape(STATE, width)
    table = pltpu.VMEM((ring, heads, LANES), F32)
    y, read_out, scale = call(
        scan_kernel,
        (struct(blocks, F32), struct((ring, rows, STATE), BF16), struct(blocks, F32)),
        [pltpu.VMEM((STATE, width), F32), pltpu.VMEM((ring, LANES, LANES), F32), table, table],
        (x, read_in, *out_pieces, steps, bias, rate, jnp.repeat(skip_gain, HEAD_DIM).reshape(1, width)),
        (10000000000, 8000000),
    )
    y = call(carry_kernel, struct(blocks, BF16), [], (y, read_out, scale, incoming), (3000000000, 6000000))
    y = lax.all_to_all(y, "fsdp", 0, 0)

    return pl.pallas_call(
        finish_kernel,
        grid=(GROUPS,),
        out_shape=struct(ssm_input.shape, BF16),
        in_specs=[
            pl.BlockSpec((ring // GROUPS, rows, width), lambda g: (g, 0, 0)),
            pl.BlockSpec((rows, group_width), lambda g: (0, g)),
            pl.BlockSpec((1, group_width), lambda g: (0, g)),
        ],
        out_specs=pl.BlockSpec((rows, group_width), lambda g: (0, g)),
        scratch_shapes=[pltpu.VMEM((rows, group_width), F32)],
        compiler_params=params,
    )(y, gate_input, norm_gain.reshape(1, -1))


def solution(mesh):
    return jax.shard_map(
        local,
        mesh=mesh,
        in_specs=(
            P(("batch", "seq", "fsdp"), None),
            P(("batch", "seq", "fsdp"), None),
            P(("batch", "seq", "fsdp"), None),
            P(("batch", "seq", "fsdp"), None),
            P(None, "fsdp"),
            P(None, "fsdp"),
            P("fsdp"),
            P("fsdp"),
            P("fsdp"),
            P(),
        ),
        out_specs=P(("batch", "seq", "fsdp"), None),
        check_vma=False,
    )
```

```python
import jax
import jax.numpy as jnp
from jax import lax
from jax.experimental import pallas as pl
from jax.experimental.pallas import tpu as pltpu
from jax.sharding import PartitionSpec as P

HEAD_DIM = 64
STATE = 256
GROUPS = 4
LANES = 128
HALO = 8
LOG2E = 1.4426950408889634

F32 = jnp.float32
BF16 = jnp.bfloat16
exact = lax.Precision.HIGHEST
params = pltpu.CompilerParams(vmem_limit_bytes=48 * 2**20)
wide = pltpu.CompilerParams(vmem_limit_bytes=60 * 2**20)


def iota(shape, dim):
    return lax.broadcasted_iota(jnp.int32, shape, dim)


def decay_tables(steps_ref, bias_ref, log_rate_ref, rows):
    count, heads, lanes = steps_ref.shape
    dt = jax.nn.softplus(steps_ref[...] + bias_ref[...][None])
    log_decay = -jnp.exp(log_rate_ref[...])[None] * dt
    size = (lanes, lanes)
    upper = jnp.where(iota(size, 0) <= iota(size, 1), 1.0, 0.0).astype(F32)
    flat = log_decay.reshape(count * heads, lanes)
    cum = jnp.dot(flat, upper, precision=exact, preferred_element_type=F32)
    return dt.reshape(count * heads, lanes), cum, cum[:, rows - 1 : rows]


def sums_of_others(cum, rows, heads, later):
    size = (cum.shape[0], cum.shape[0])
    mine, other = iota(size, 0), iota(size, 1)
    beyond = other // heads > mine // heads if later else other // heads < mine // heads
    chosen = jnp.where((mine % heads == other % heads) & beyond, 1.0, 0.0).astype(F32)
    return jnp.dot(chosen, cum, precision=exact, preferred_element_type=F32)[:, rows - 1 : rows]


def high_low(table):
    high = table.astype(BF16).astype(F32)
    return high, table - high


def spread_matrix(heads, width, copy):
    shape = (LANES, width)
    row, lane = iota(shape, 0), iota(shape, 1)
    ours = (row >= copy * heads) & (row < (copy + 2) * heads) & (row % heads == lane // HEAD_DIM)
    return jnp.where(ours, 1.0, 0.0).astype(BF16)


def fill(table, parts):
    table[...] = jnp.zeros(table.shape, F32)
    count, _, lanes = table.shape
    for k, part in enumerate(parts):
        heads = part.shape[0] // count
        table[:, k * heads : (k + 1) * heads] = part.reshape(count, heads, lanes)


def silu_conv(scratch, block, taps):
    rows = block.shape[0] - HALO
    scratch[...] = block
    total = scratch[HALO - 3 : HALO - 3 + rows] * taps[0:1]
    for k in range(1, 4):
        total = total + scratch[HALO - 3 + k : HALO - 3 + k + rows] * taps[k : k + 1]
    return jax.nn.silu(total)


def turned(block):
    return pltpu.roll(block, HEAD_DIM, 1)


def pack_kernel(x_ref, b_ref, c_ref, steps_ref, x_tail_ref, b_tail_ref, c_tail_ref, taps_ref, out_ref, turned_steps):
    count, _, lanes = out_ref.shape
    width = lanes - LANES
    rows = x_ref.shape[0]
    g = pl.program_id(0)
    heads = steps_ref.shape[1] // GROUPS // count
    left = iota((HALO + rows, LANES), 1) < HEAD_DIM
    below = iota((HALO, width), 0) >= HALO - 3
    below_c = iota((HALO, LANES), 0) >= HALO - 3

    @pl.when(g == 0)
    def _():
        steps = steps_ref[...].astype(F32)
        turned_steps[...] = jnp.transpose(
            jnp.concatenate([steps, jnp.zeros((LANES - rows, steps.shape[1]), F32)], axis=0)
        )

    own_taps = taps_ref[...].astype(F32)
    for j in range(count):
        own = turned_steps[pl.ds(pl.multiple_of((g * count + j) * heads, heads), heads)]
        top = jnp.concatenate([own[:4], own[4:], jnp.zeros((4, width - 2 * LANES), F32)], axis=1)
        top = jnp.concatenate([top, jnp.zeros((HALO - 4, width), F32)], axis=0)
        lanes_j = slice(j * width, (j + 1) * width)
        top = jnp.where(below, x_tail_ref[:, lanes_j].astype(F32), top)
        out_ref[j, :, :width] = jnp.concatenate([top, x_ref[:, lanes_j].astype(F32)], axis=0).astype(BF16)
        taps = own_taps if j % 2 == 0 else turned(own_taps)
        taps = jnp.concatenate([taps, jnp.zeros((HALO - 4, LANES), F32)], axis=0)
        half = slice(j // 2 * LANES, (j // 2 + 1) * LANES)
        b = jnp.concatenate([b_tail_ref[:, half].astype(F32), b_ref[:, half].astype(F32)], axis=0)
        c = jnp.concatenate([c_tail_ref[:, half].astype(F32), c_ref[:, half].astype(F32)], axis=0)
        both = jnp.where(left, b, turned(c)) if j % 2 == 0 else jnp.where(left, turned(b), c)
        both = jnp.concatenate([jnp.where(below_c, both[:HALO], taps), both[HALO:]], axis=0)
        out_ref[j, :, width:] = both.astype(BF16)


def coupling_kernel(from_ref, m_ref, b_ref, c_ref, steps_ref, scratch):
    count, _, lanes = m_ref.shape
    width = lanes - LANES
    rows = m_ref.shape[1] - HALO
    taps_b = m_ref[from_ref[0], :, width:].astype(F32)[:4]
    taps_c = turned(m_ref[from_ref[1], :, width:].astype(F32)[:4])
    taps = jnp.where(iota((4, LANES), 1) < HEAD_DIM, taps_b, taps_c)
    left = iota((rows // 2, LANES), 1) < HEAD_DIM

    def body(c, _):
        steps = m_ref[c, :, : 2 * LANES].astype(F32)
        steps_ref[c] = jnp.concatenate([steps[:4, :LANES], steps[:4, LANES:]], axis=0)
        both = silu_conv(scratch, m_ref[c, :, width:].astype(F32), taps)
        early, late = both[: rows // 2], both[rows // 2 :]
        b_ref[c] = jnp.where(left, early, turned(late)).astype(BF16)
        c_ref[c] = jnp.where(left, turned(early), late).astype(BF16)
        return 0

    lax.fori_loop(0, count, body, 0, unroll=4)


def unpacked(pieces):
    early, late = [], []
    for k in range(0, 4, 2):
        a, b = pieces[k].astype(F32), pieces[k + 1].astype(F32)
        left = iota(a.shape, 1) < HEAD_DIM
        early.append(jnp.where(left, a, turned(b)))
        late.append(jnp.where(left, turned(a), b))
    whole = jnp.concatenate([jnp.concatenate(early, axis=1), jnp.concatenate(late, axis=1)], axis=0)
    return whole.astype(BF16)


def input_kernel(m_ref, taps_ref, steps_ref, bias_ref, log_rate_ref, x_ref, weighted_ref, total_ref, scratch, table):
    count, rows, width = x_ref.shape
    heads = steps_ref.shape[1]
    dt, cum, tot = decay_tables(steps_ref, bias_ref, log_rate_ref, rows)
    later = sums_of_others(cum, rows, heads, True)
    fill(table, high_low(jnp.exp(later + (tot - cum)) * dt))
    own = iota((heads, width), 0) == iota((heads, width), 1) // HEAD_DIM
    section = jnp.broadcast_to(tot[0:heads] + later[0:heads, 0:1], own.shape)
    logs = jnp.sum(jnp.where(own, section, 0.0), axis=0, keepdims=True)
    total_ref[...] = jnp.broadcast_to(logs, total_ref.shape)
    taps = taps_ref[...].astype(F32)
    spread = spread_matrix(heads, width, 0)

    def body(c, _):
        x = silu_conv(scratch, m_ref[c, :, :width].astype(F32), taps).astype(BF16)
        x_ref[c] = x
        columns = jnp.transpose(table[c])[:rows].astype(BF16)
        scale = jnp.dot(columns, spread, preferred_element_type=F32)
        weighted_ref[c] = (x.astype(F32) * scale).astype(BF16)
        return 0

    lax.fori_loop(0, count, body, 0, unroll=4)


def state_kernel(p0, p1, p2, p3, weighted_ref, logs_ref, state_ref, in_ref):
    count, rows, width = weighted_ref.shape
    sections, share_rows, _ = state_ref.shape

    def body(c, _):
        in_ref[c] = unpacked([p[c] for p in (p0, p1, p2, p3)])
        return 0

    lax.fori_loop(0, count, body, 0, unroll=4)
    state = lax.dot_general(
        in_ref[...].reshape(count * rows, STATE),
        weighted_ref[...].reshape(count * rows, width),
        (((0,), (0,)), ((), ())),
        preferred_element_type=F32,
    )
    high, low = high_low(logs_ref[...])
    logs = jnp.where(iota(high.shape, 0) == 0, high, low)
    share = STATE // sections
    for s in range(sections):
        block = jnp.concatenate([state[s * share : (s + 1) * share], logs], axis=0)
        state_ref[s] = block.astype(BF16)


def relay_kernel(state_ref, out_ref):
    share = out_ref.shape[1]
    carried = jnp.zeros(out_ref.shape[1:], F32)
    for s in range(state_ref.shape[0]):
        out_ref[s] = carried.astype(BF16)
        block = state_ref[s].astype(F32)
        decay = jnp.exp(block[share : share + 1] + block[share + 1 : share + 2])
        carried = decay * carried + block[:share]


def scan_kernel(x_ref, in_ref, p0, p1, p2, p3, steps_ref, bias_ref, log_rate_ref, skip_ref,
                y_ref, out_ref, scale_ref, state, table, column_logs, row_logs):
    count, rows, width = x_ref.shape
    heads = steps_ref.shape[1]
    dt, cum, tot = decay_tables(steps_ref, bias_ref, log_rate_ref, rows)
    blocked = (count, heads, dt.shape[1])
    earlier = sums_of_others(cum, rows, heads, False)
    fill(table, high_low(jnp.exp(tot - cum) * dt) + high_low(jnp.exp(cum)) + high_low(jnp.exp(earlier + cum)))
    column_logs[...] = (cum * LOG2E).reshape(blocked)
    row_logs[...] = ((jnp.log(dt) - cum) * LOG2E).reshape(blocked)
    spread_in, spread_out, spread_all = (spread_matrix(heads, width, k) for k in (0, 2, 4))
    skip = skip_ref[...]
    state[...] = jnp.zeros(state.shape, F32)
    causal = iota((rows, rows), 0) >= iota((rows, rows), 1)
    left = iota((rows, LANES), 1) < HEAD_DIM

    def body(c, _):
        q = unpacked([p[c] for p in (p0, p1, p2, p3)])
        out_ref[c] = q
        b, x = in_ref[c], x_ref[c]
        meet = lax.dot_general(q, b, (((1,), (1,)), ((), ())), preferred_element_type=F32)
        meet = jnp.where(causal, meet, 0.0)
        columns = jnp.transpose(table[c])[:rows].astype(BF16)
        scale_in = jnp.dot(columns, spread_in, preferred_element_type=F32)
        scale_out = jnp.dot(columns, spread_out, preferred_element_type=F32)
        scale_ref[c] = jnp.dot(columns, spread_all, preferred_element_type=F32)
        logs = jnp.transpose(column_logs[c])[:rows]
        rows_c = row_logs[c]
        carried = jnp.dot(q, state[...].astype(BF16), preferred_element_type=F32) * scale_out
        x32 = x.astype(F32)
        for pair in range(width // LANES):
            lanes = slice(pair * LANES, (pair + 1) * LANES)
            both = []
            for k in range(2):
                h = 2 * pair + k
                mix = jnp.exp2(logs[:, h : h + 1] + rows_c[h : h + 1, :rows]) * meet
                both.append(jnp.dot(mix.astype(BF16), x[:, lanes], preferred_element_type=F32))
            mixed = jnp.where(left, both[0], both[1])
            y_ref[c, :, lanes] = mixed + carried[:, lanes] + skip[:, lanes] * x32[:, lanes]
        state[...] = state[...] * scale_out[rows - 1 : rows] + lax.dot_general(
            b, (x32 * scale_in).astype(BF16), (((0,), (0,)), ((), ())), preferred_element_type=F32
        )
        return 0

    lax.fori_loop(0, count, body, 0, unroll=4)


def carry_kernel(y_ref, out_ref, scale_ref, incoming_ref, sum_ref):
    incoming = incoming_ref[...]

    def body(c, _):
        carried = jnp.dot(out_ref[c], incoming, preferred_element_type=F32)
        sum_ref[c] = (y_ref[c] + carried * scale_ref[c]).astype(BF16)
        return 0

    lax.fori_loop(0, y_ref.shape[0], body, 0, unroll=4)


def finish_kernel(*refs):
    parts, (gate_ref, gain_ref, out_ref, gated_ref) = refs[:-4], refs[-4:]
    blocks, rows, width = parts[0].shape
    total = jnp.zeros((rows, 1), F32)
    pieces = [(z, p) for z in range(blocks) for p in range(len(parts))]
    for i, (z, p) in enumerate(pieces):
        lanes = slice(i * width, (i + 1) * width)
        gated = parts[p][z].astype(F32) * jax.nn.silu(gate_ref[:, lanes].astype(F32))
        gated_ref[:, lanes] = gated
        total = total + jnp.sum(gated * gated, axis=1, keepdims=True)
    scale = lax.rsqrt(total / (len(pieces) * width) + 1e-05)
    for i in range(len(pieces)):
        lanes = slice(i * width, (i + 1) * width)
        out_ref[:, lanes] = (gated_ref[:, lanes] * scale * gain_ref[:, lanes].astype(F32)).astype(BF16)


def call(kernel, outs, scratch, args, cost=(0, 0), smem_first=False):
    specs = [pl.BlockSpec(memory_space=pltpu.VMEM)] * len(args)
    if smem_first:
        specs[0] = pl.BlockSpec(memory_space=pltpu.SMEM)
    return pl.pallas_call(
        kernel,
        out_shape=outs,
        in_specs=specs,
        out_specs=jax.tree.map(lambda _: pl.BlockSpec(memory_space=pltpu.VMEM), outs),
        scratch_shapes=scratch,
        compiler_params=params,
        cost_estimate=pl.CostEstimate(flops=cost[0], bytes_accessed=cost[1], transcendentals=0),
    )(*args)


def local(
    ssm_input,
    gate_input,
    coupling,
    step_input,
    conv_input,
    conv_coupling,
    step_bias,
    log_rate,
    skip_gain,
    norm_gain,
):
    rows, channels = ssm_input.shape
    ring = lax.axis_size("fsdp")
    seq = lax.axis_size("seq")
    heads = step_bias.shape[0]
    width = conv_input.shape[1]
    struct = jax.ShapeDtypeStruct
    place = lax.axis_index("fsdp").astype(jnp.int32)
    bias, rate = step_bias.reshape(heads, 1), log_rate.reshape(heads, 1)

    route = [(i, i + 1) for i in range(seq * ring - 1)]
    last_rows = jnp.concatenate([ssm_input[rows - HALO :], coupling[rows - HALO :]], axis=1)
    tails = lax.ppermute(last_rows, ("seq", "fsdp"), route)
    group_width = channels // GROUPS

    def columns_of(count, size, first):
        return pl.BlockSpec((count, size), lambda g: (0, first + g))

    def same(*shape):
        return pl.BlockSpec(shape, lambda g: (0,) * len(shape))

    message = pl.pallas_call(
        pack_kernel,
        grid=(GROUPS,),
        out_shape=struct((ring, HALO + rows, width + LANES), BF16),
        in_specs=[
            columns_of(rows, group_width, 0),
            columns_of(rows, STATE, 0),
            columns_of(rows, STATE, GROUPS),
            same(*step_input.shape),
            columns_of(HALO, group_width, 0),
            columns_of(HALO, STATE, channels // STATE),
            columns_of(HALO, STATE, channels // STATE + GROUPS),
            same(*conv_coupling.shape),
        ],
        out_specs=pl.BlockSpec((ring // GROUPS, HALO + rows, width + LANES), lambda g: (g, 0, 0)),
        scratch_shapes=[pltpu.VMEM((LANES, LANES), F32)],
        compiler_params=wide,
    )(ssm_input, coupling, coupling, step_input, tails, tails, tails, conv_coupling)
    message = lax.all_to_all(message, "fsdp", 0, 0)

    senders = 2 * (place // 4) + place % 4 // 2 + jnp.array([0, 2 * GROUPS], jnp.int32)
    packed = struct((ring, rows // 2, LANES), BF16)
    own_in, own_out, steps = call(
        coupling_kernel,
        (packed, packed, struct((ring, heads, LANES), F32)),
        [pltpu.VMEM((HALO + rows, LANES), F32)],
        (senders, message),
        (4000000, 3000000),
        True,
    )
    pieces = [own_in] + [lax.ppermute(own_in, "fsdp", [(i, i ^ d) for i in range(ring)]) for d in range(1, 4)]
    blocks = (ring, rows, width)
    x, weighted, logs = call(
        input_kernel,
        (struct(blocks, BF16), struct(blocks, BF16), struct((8, width), F32)),
        [pltpu.VMEM((HALO + rows, width), F32), pltpu.VMEM((ring, LANES, LANES), F32)],
        (message, conv_input, steps, bias, rate),
        (6000000000, 6000000),
    )
    nearest = lax.ppermute(own_out, "fsdp", [(i, i ^ 1) for i in range(ring)])
    own_out, nearest, weighted = lax.optimization_barrier((own_out, nearest, weighted))
    out_pieces = [own_out, nearest] + [lax.ppermute(own_out, "fsdp", [(i, i ^ d) for i in range(ring)]) for d in (2, 3)]
    share = STATE // seq
    state, read_in = call(
        state_kernel,
        (struct((seq, share + 8, width), BF16), struct((ring, rows, STATE), BF16)),
        [],
        (*pieces, weighted, logs),
        (2000000000, 5000000),
    )
    state = lax.all_to_all(state, "seq", 0, 0)
    incoming = call(relay_kernel, struct((seq, share, width), BF16), [], (state,), (500000000, 600000))
    incoming = lax.all_to_all(incoming, "seq", 0, 0).reshape(STATE, width)
    table = pltpu.VMEM((ring, heads, LANES), F32)
    y, read_out, scale = call(
        scan_kernel,
        (struct(blocks, F32), struct((ring, rows, STATE), BF16), struct(blocks, F32)),
        [pltpu.VMEM((STATE, width), F32), pltpu.VMEM((ring, LANES, LANES), F32), table, table],
        (x, read_in, *out_pieces, steps, bias, rate, jnp.repeat(skip_gain, HEAD_DIM).reshape(1, width)),
        (10000000000, 8000000),
    )
    some = ring // 4
    y = pl.pallas_call(
        carry_kernel,
        grid=(4,),
        out_shape=struct(blocks, BF16),
        in_specs=[
            pl.BlockSpec((some, rows, width), lambda i: (i, 0, 0)),
            pl.BlockSpec((some, rows, STATE), lambda i: (i, 0, 0)),
            pl.BlockSpec((some, rows, width), lambda i: (i, 0, 0)),
            same(STATE, width),
        ],
        out_specs=pl.BlockSpec((some, rows, width), lambda i: (i, 0, 0)),
        compiler_params=wide,
    )(y, read_out, scale, incoming)
    y = lax.all_to_all(y, "fsdp", 0, 0)

    return pl.pallas_call(
        finish_kernel,
        grid=(GROUPS,),
        out_shape=struct(ssm_input.shape, BF16),
        in_specs=[
            pl.BlockSpec((ring // GROUPS, rows, width), lambda g: (g, 0, 0)),
            pl.BlockSpec((rows, group_width), lambda g: (0, g)),
            pl.BlockSpec((1, group_width), lambda g: (0, g)),
        ],
        out_specs=pl.BlockSpec((rows, group_width), lambda g: (0, g)),
        scratch_shapes=[pltpu.VMEM((rows, group_width), F32)],
        compiler_params=params,
    )(y, gate_input, norm_gain.reshape(1, -1))


def solution(mesh):
    return jax.shard_map(
        local,
        mesh=mesh,
        in_specs=(
            P(("batch", "seq", "fsdp"), None),
            P(("batch", "seq", "fsdp"), None),
            P(("batch", "seq", "fsdp"), None),
            P(("batch", "seq", "fsdp"), None),
            P(None, "fsdp"),
            P(None, "fsdp"),
            P("fsdp"),
            P("fsdp"),
            P("fsdp"),
            P(),
        ),
        out_specs=P(("batch", "seq", "fsdp"), None),
        check_vma=False,
    )
```

```python
import jax
import jax.numpy as jnp
from jax import lax
from jax.experimental import pallas as pl
from jax.experimental.pallas import tpu as pltpu
from jax.sharding import PartitionSpec as P

HEAD_DIM = 64
STATE = 256
GROUPS = 4
LANES = 128
HALO = 8
LOG2E = 1.4426950408889634

F32 = jnp.float32
BF16 = jnp.bfloat16
exact = lax.Precision.HIGHEST
params = pltpu.CompilerParams(vmem_limit_bytes=50 * 2**20)
wide = pltpu.CompilerParams(vmem_limit_bytes=60 * 2**20)


def iota(shape, dim):
    return lax.broadcasted_iota(jnp.int32, shape, dim)


def decay_tables(steps_ref, bias_ref, log_rate_ref, rows):
    count, heads, lanes = steps_ref.shape
    dt = jax.nn.softplus(steps_ref[...] + bias_ref[...][None])
    log_decay = -jnp.exp(log_rate_ref[...])[None] * dt
    size = (lanes, lanes)
    upper = jnp.where(iota(size, 0) <= iota(size, 1), 1.0, 0.0).astype(F32)
    flat = log_decay.reshape(count * heads, lanes)
    cum = jnp.dot(flat, upper, precision=exact, preferred_element_type=F32)
    return dt.reshape(count * heads, lanes), cum, cum[:, rows - 1 : rows]


def sums_of_others(cum, rows, heads, later):
    size = (cum.shape[0], cum.shape[0])
    mine, other = iota(size, 0), iota(size, 1)
    beyond = other // heads > mine // heads if later else other // heads < mine // heads
    chosen = jnp.where((mine % heads == other % heads) & beyond, 1.0, 0.0).astype(F32)
    return jnp.dot(chosen, cum, precision=exact, preferred_element_type=F32)[:, rows - 1 : rows]


def high_low(table):
    high = table.astype(BF16).astype(F32)
    return high, table - high


def spread_matrix(heads, width, copy):
    shape = (LANES, width)
    row, lane = iota(shape, 0), iota(shape, 1)
    ours = (row >= copy * heads) & (row < (copy + 2) * heads) & (row % heads == lane // HEAD_DIM)
    return jnp.where(ours, 1.0, 0.0).astype(BF16)


def fill(table, parts):
    table[...] = jnp.zeros(table.shape, F32)
    count, _, lanes = table.shape
    for k, part in enumerate(parts):
        heads = part.shape[0] // count
        table[:, k * heads : (k + 1) * heads] = part.reshape(count, heads, lanes)


def silu_conv(scratch, block, taps):
    rows = block.shape[0] - HALO
    scratch[...] = block
    total = scratch[HALO - 3 : HALO - 3 + rows] * taps[0:1]
    for k in range(1, 4):
        total = total + scratch[HALO - 3 + k : HALO - 3 + k + rows] * taps[k : k + 1]
    return jax.nn.silu(total)


def turned(block):
    return pltpu.roll(block, HEAD_DIM, 1)


def pack_kernel(x_ref, b_ref, c_ref, steps_ref, x_tail_ref, b_tail_ref, c_tail_ref, taps_ref, out_ref, turned_steps):
    count, _, lanes = out_ref.shape
    width = lanes - LANES
    rows = x_ref.shape[0]
    g = pl.program_id(0)
    heads = steps_ref.shape[1] // GROUPS // count
    left = iota((HALO + rows, LANES), 1) < HEAD_DIM
    below = iota((HALO, width), 0) >= HALO - 3
    below_c = iota((HALO, LANES), 0) >= HALO - 3

    @pl.when(g == 0)
    def _():
        steps = steps_ref[...].astype(F32)
        turned_steps[...] = jnp.transpose(
            jnp.concatenate([steps, jnp.zeros((LANES - rows, steps.shape[1]), F32)], axis=0)
        )

    own_taps = taps_ref[...].astype(F32)
    for j in range(count):
        own = turned_steps[pl.ds(pl.multiple_of((g * count + j) * heads, heads), heads)]
        top = jnp.concatenate([own[:4], own[4:], jnp.zeros((4, width - 2 * LANES), F32)], axis=1)
        top = jnp.concatenate([top, jnp.zeros((HALO - 4, width), F32)], axis=0)
        lanes_j = slice(j * width, (j + 1) * width)
        top = jnp.where(below, x_tail_ref[:, lanes_j].astype(F32), top)
        out_ref[j, :, :width] = jnp.concatenate([top, x_ref[:, lanes_j].astype(F32)], axis=0).astype(BF16)
        taps = own_taps if j % 2 == 0 else turned(own_taps)
        taps = jnp.concatenate([taps, jnp.zeros((HALO - 4, LANES), F32)], axis=0)
        half = slice(j // 2 * LANES, (j // 2 + 1) * LANES)
        b = jnp.concatenate([b_tail_ref[:, half].astype(F32), b_ref[:, half].astype(F32)], axis=0)
        c = jnp.concatenate([c_tail_ref[:, half].astype(F32), c_ref[:, half].astype(F32)], axis=0)
        both = jnp.where(left, b, turned(c)) if j % 2 == 0 else jnp.where(left, turned(b), c)
        both = jnp.concatenate([jnp.where(below_c, both[:HALO], taps), both[HALO:]], axis=0)
        out_ref[j, :, width:] = both.astype(BF16)


def coupling_kernel(from_ref, m_ref, b_ref, c_ref, steps_ref, scratch):
    count, _, lanes = m_ref.shape
    width = lanes - LANES
    rows = m_ref.shape[1] - HALO
    taps_b = m_ref[from_ref[0], :, width:].astype(F32)[:4]
    taps_c = turned(m_ref[from_ref[1], :, width:].astype(F32)[:4])
    taps = jnp.where(iota((4, LANES), 1) < HEAD_DIM, taps_b, taps_c)
    left = iota((rows // 2, LANES), 1) < HEAD_DIM

    def body(c, _):
        steps = m_ref[c, :, : 2 * LANES].astype(F32)
        steps_ref[c] = jnp.concatenate([steps[:4, :LANES], steps[:4, LANES:]], axis=0)
        both = silu_conv(scratch, m_ref[c, :, width:].astype(F32), taps)
        early, late = both[: rows // 2], both[rows // 2 :]
        b_ref[c] = jnp.where(left, early, turned(late)).astype(BF16)
        c_ref[c] = jnp.where(left, turned(early), late).astype(BF16)
        return 0

    lax.fori_loop(0, count, body, 0, unroll=4)


def unpacked(pieces):
    early, late = [], []
    for k in range(0, 4, 2):
        a, b = pieces[k].astype(F32), pieces[k + 1].astype(F32)
        left = iota(a.shape, 1) < HEAD_DIM
        early.append(jnp.where(left, a, turned(b)))
        late.append(jnp.where(left, turned(a), b))
    whole = jnp.concatenate([jnp.concatenate(early, axis=1), jnp.concatenate(late, axis=1)], axis=0)
    return whole.astype(BF16)


def input_kernel(m_ref, taps_ref, steps_ref, bias_ref, log_rate_ref, x_ref, weighted_ref, total_ref, scratch, table):
    count, rows, width = x_ref.shape
    heads = steps_ref.shape[1]
    dt, cum, tot = decay_tables(steps_ref, bias_ref, log_rate_ref, rows)
    later = sums_of_others(cum, rows, heads, True)
    fill(table, high_low(jnp.exp(later + (tot - cum)) * dt))
    own = iota((heads, width), 0) == iota((heads, width), 1) // HEAD_DIM
    section = jnp.broadcast_to(tot[0:heads] + later[0:heads, 0:1], own.shape)
    logs = jnp.sum(jnp.where(own, section, 0.0), axis=0, keepdims=True)
    total_ref[...] = jnp.broadcast_to(logs, total_ref.shape)
    taps = taps_ref[...].astype(F32)
    spread = spread_matrix(heads, width, 0)

    def body(c, _):
        x = silu_conv(scratch, m_ref[c, :, :width].astype(F32), taps).astype(BF16)
        x_ref[c] = x
        columns = jnp.transpose(table[c])[:rows].astype(BF16)
        scale = jnp.dot(columns, spread, preferred_element_type=F32)
        weighted_ref[c] = (x.astype(F32) * scale).astype(BF16)
        return 0

    lax.fori_loop(0, count, body, 0, unroll=4)


def state_kernel(p0, p1, p2, p3, weighted_ref, logs_ref, state_ref, in_ref):
    count, rows, width = weighted_ref.shape
    sections, share_rows, _ = state_ref.shape

    def body(c, _):
        in_ref[c] = unpacked([p[c] for p in (p0, p1, p2, p3)])
        return 0

    lax.fori_loop(0, count, body, 0, unroll=4)
    state = lax.dot_general(
        in_ref[...].reshape(count * rows, STATE),
        weighted_ref[...].reshape(count * rows, width),
        (((0,), (0,)), ((), ())),
        preferred_element_type=F32,
    )
    high, low = high_low(logs_ref[...])
    logs = jnp.where(iota(high.shape, 0) == 0, high, low)
    share = STATE // sections
    for s in range(sections):
        block = jnp.concatenate([state[s * share : (s + 1) * share], logs], axis=0)
        state_ref[s] = block.astype(BF16)


def relay_kernel(state_ref, out_ref):
    share = out_ref.shape[1]
    carried = jnp.zeros(out_ref.shape[1:], F32)
    for s in range(state_ref.shape[0]):
        out_ref[s] = carried.astype(BF16)
        block = state_ref[s].astype(F32)
        decay = jnp.exp(block[share : share + 1] + block[share + 1 : share + 2])
        carried = decay * carried + block[:share]


def scan_kernel(x_ref, in_ref, p0, p1, p2, p3, steps_ref, bias_ref, log_rate_ref, skip_ref,
                y_ref, out_ref, scale_ref, state, table, column_logs, row_logs):
    count, rows, width = x_ref.shape
    heads = steps_ref.shape[1]
    dt, cum, tot = decay_tables(steps_ref, bias_ref, log_rate_ref, rows)
    blocked = (count, heads, dt.shape[1])
    earlier = sums_of_others(cum, rows, heads, False)
    fill(table, high_low(jnp.exp(tot - cum) * dt) + high_low(jnp.exp(cum)) + high_low(jnp.exp(earlier + cum)))
    column_logs[...] = (cum * LOG2E).reshape(blocked)
    row_logs[...] = ((jnp.log(dt) - cum) * LOG2E).reshape(blocked)
    spread_in, spread_out, spread_all = (spread_matrix(heads, width, k) for k in (0, 2, 4))
    skip = skip_ref[...]
    state[...] = jnp.zeros(state.shape, F32)
    causal = iota((rows, rows), 0) >= iota((rows, rows), 1)
    left = iota((rows, LANES), 1) < HEAD_DIM

    def body(c, _):
        q = unpacked([p[c] for p in (p0, p1, p2, p3)])
        out_ref[c] = q
        b, x = in_ref[c], x_ref[c]
        meet = lax.dot_general(q, b, (((1,), (1,)), ((), ())), preferred_element_type=F32)
        meet = jnp.where(causal, meet, 0.0)
        columns = jnp.transpose(table[c])[:rows].astype(BF16)
        scale_in = jnp.dot(columns, spread_in, preferred_element_type=F32)
        scale_out = jnp.dot(columns, spread_out, preferred_element_type=F32)
        scale_ref[c] = jnp.dot(columns, spread_all, preferred_element_type=F32)
        logs = jnp.transpose(column_logs[c])[:rows]
        rows_c = row_logs[c]
        carried = jnp.dot(q, state[...].astype(BF16), preferred_element_type=F32) * scale_out
        x32 = x.astype(F32)
        for pair in range(width // LANES):
            lanes = slice(pair * LANES, (pair + 1) * LANES)
            both = []
            for k in range(2):
                h = 2 * pair + k
                mix = jnp.exp2(logs[:, h : h + 1] + rows_c[h : h + 1, :rows]) * meet
                both.append(jnp.dot(mix.astype(BF16), x[:, lanes], preferred_element_type=F32))
            mixed = jnp.where(left, both[0], both[1])
            y_ref[c, :, lanes] = mixed + carried[:, lanes] + skip[:, lanes] * x32[:, lanes]
        state[...] = state[...] * scale_out[rows - 1 : rows] + lax.dot_general(
            b, (x32 * scale_in).astype(BF16), (((0,), (0,)), ((), ())), preferred_element_type=F32
        )
        return 0

    lax.fori_loop(0, count, body, 0, unroll=8)


def carry_kernel(y_ref, out_ref, scale_ref, incoming_ref, sum_ref):
    incoming = incoming_ref[...]

    def body(c, _):
        carried = jnp.dot(out_ref[c], incoming, preferred_element_type=F32)
        sum_ref[c] = (y_ref[c] + carried * scale_ref[c]).astype(BF16)
        return 0

    lax.fori_loop(0, y_ref.shape[0], body, 0, unroll=4)


def finish_kernel(*refs):
    parts, (gate_ref, gain_ref, out_ref, gated_ref) = refs[:-4], refs[-4:]
    blocks, rows, width = parts[0].shape
    total = jnp.zeros((rows, 1), F32)
    pieces = [(z, p) for z in range(blocks) for p in range(len(parts))]
    for i, (z, p) in enumerate(pieces):
        lanes = slice(i * width, (i + 1) * width)
        gated = parts[p][z].astype(F32) * jax.nn.silu(gate_ref[:, lanes].astype(F32))
        gated_ref[:, lanes] = gated
        total = total + jnp.sum(gated * gated, axis=1, keepdims=True)
    scale = lax.rsqrt(total / (len(pieces) * width) + 1e-05)
    for i in range(len(pieces)):
        lanes = slice(i * width, (i + 1) * width)
        out_ref[:, lanes] = (gated_ref[:, lanes] * scale * gain_ref[:, lanes].astype(F32)).astype(BF16)


def call(kernel, outs, scratch, args, cost=(0, 0), smem_first=False):
    specs = [pl.BlockSpec(memory_space=pltpu.VMEM)] * len(args)
    if smem_first:
        specs[0] = pl.BlockSpec(memory_space=pltpu.SMEM)
    return pl.pallas_call(
        kernel,
        out_shape=outs,
        in_specs=specs,
        out_specs=jax.tree.map(lambda _: pl.BlockSpec(memory_space=pltpu.VMEM), outs),
        scratch_shapes=scratch,
        compiler_params=params,
        cost_estimate=pl.CostEstimate(flops=cost[0], bytes_accessed=cost[1], transcendentals=0),
    )(*args)


def local(
    ssm_input,
    gate_input,
    coupling,
    step_input,
    conv_input,
    conv_coupling,
    step_bias,
    log_rate,
    skip_gain,
    norm_gain,
):
    rows, channels = ssm_input.shape
    ring = lax.axis_size("fsdp")
    seq = lax.axis_size("seq")
    heads = step_bias.shape[0]
    width = conv_input.shape[1]
    struct = jax.ShapeDtypeStruct
    place = lax.axis_index("fsdp").astype(jnp.int32)
    bias, rate = step_bias.reshape(heads, 1), log_rate.reshape(heads, 1)

    route = [(i, i + 1) for i in range(seq * ring - 1)]
    last_rows = jnp.concatenate([ssm_input[rows - HALO :], coupling[rows - HALO :]], axis=1)
    tails = lax.ppermute(last_rows, ("seq", "fsdp"), route)
    group_width = channels // GROUPS

    def columns_of(count, size, first):
        return pl.BlockSpec((count, size), lambda g: (0, first + g))

    def same(*shape):
        return pl.BlockSpec(shape, lambda g: (0,) * len(shape))

    message = pl.pallas_call(
        pack_kernel,
        grid=(GROUPS,),
        out_shape=struct((ring, HALO + rows, width + LANES), BF16),
        in_specs=[
            columns_of(rows, group_width, 0),
            columns_of(rows, STATE, 0),
            columns_of(rows, STATE, GROUPS),
            same(*step_input.shape),
            columns_of(HALO, group_width, 0),
            columns_of(HALO, STATE, channels // STATE),
            columns_of(HALO, STATE, channels // STATE + GROUPS),
            same(*conv_coupling.shape),
        ],
        out_specs=pl.BlockSpec((ring // GROUPS, HALO + rows, width + LANES), lambda g: (g, 0, 0)),
        scratch_shapes=[pltpu.VMEM((LANES, LANES), F32)],
        compiler_params=wide,
    )(ssm_input, coupling, coupling, step_input, tails, tails, tails, conv_coupling)
    message = lax.all_to_all(message, "fsdp", 0, 0)

    senders = 2 * (place // 4) + place % 4 // 2 + jnp.array([0, 2 * GROUPS], jnp.int32)
    packed = struct((ring, rows // 2, LANES), BF16)
    own_in, own_out, steps = call(
        coupling_kernel,
        (packed, packed, struct((ring, heads, LANES), F32)),
        [pltpu.VMEM((HALO + rows, LANES), F32)],
        (senders, message),
        (4000000, 3000000),
        True,
    )
    pieces = [own_in] + [lax.ppermute(own_in, "fsdp", [(i, i ^ d) for i in range(ring)]) for d in range(1, 4)]
    blocks = (ring, rows, width)
    x, weighted, logs = call(
        input_kernel,
        (struct(blocks, BF16), struct(blocks, BF16), struct((8, width), F32)),
        [pltpu.VMEM((HALO + rows, width), F32), pltpu.VMEM((ring, LANES, LANES), F32)],
        (message, conv_input, steps, bias, rate),
        (6000000000, 6000000),
    )
    own_out, weighted = lax.optimization_barrier((own_out, weighted))
    out_pieces = [own_out] + [lax.ppermute(own_out, "fsdp", [(i, i ^ d) for i in range(ring)]) for d in range(1, 4)]
    share = STATE // seq
    state, read_in = call(
        state_kernel,
        (struct((seq, share + 8, width), BF16), struct((ring, rows, STATE), BF16)),
        [],
        (*pieces, weighted, logs),
        (2000000000, 5000000),
    )
    state = lax.all_to_all(state, "seq", 0, 0)
    incoming = call(relay_kernel, struct((seq, share, width), BF16), [], (state,), (500000000, 600000))
    incoming = lax.all_to_all(incoming, "seq", 0, 0).reshape(STATE, width)
    table = pltpu.VMEM((ring, heads, LANES), F32)
    y, read_out, scale = call(
        scan_kernel,
        (struct(blocks, F32), struct((ring, rows, STATE), BF16), struct(blocks, F32)),
        [pltpu.VMEM((STATE, width), F32), pltpu.VMEM((ring, LANES, LANES), F32), table, table],
        (x, read_in, *out_pieces, steps, bias, rate, jnp.repeat(skip_gain, HEAD_DIM).reshape(1, width)),
        (10000000000, 8000000),
    )
    y = call(carry_kernel, struct(blocks, BF16), [], (y, read_out, scale, incoming), (3000000000, 6000000))
    y = lax.all_to_all(y, "fsdp", 0, 0)

    return pl.pallas_call(
        finish_kernel,
        grid=(GROUPS,),
        out_shape=struct(ssm_input.shape, BF16),
        in_specs=[
            pl.BlockSpec((ring // GROUPS, rows, width), lambda g: (g, 0, 0)),
            pl.BlockSpec((rows, group_width), lambda g: (0, g)),
            pl.BlockSpec((1, group_width), lambda g: (0, g)),
        ],
        out_specs=pl.BlockSpec((rows, group_width), lambda g: (0, g)),
        scratch_shapes=[pltpu.VMEM((rows, group_width), F32)],
        compiler_params=params,
    )(y, gate_input, norm_gain.reshape(1, -1))


def solution(mesh):
    return jax.shard_map(
        local,
        mesh=mesh,
        in_specs=(
            P(("batch", "seq", "fsdp"), None),
            P(("batch", "seq", "fsdp"), None),
            P(("batch", "seq", "fsdp"), None),
            P(("batch", "seq", "fsdp"), None),
            P(None, "fsdp"),
            P(None, "fsdp"),
            P("fsdp"),
            P("fsdp"),
            P("fsdp"),
            P(),
        ),
        out_specs=P(("batch", "seq", "fsdp"), None),
        check_vma=False,
    )
```
